128 devices in a mesh: users: 16 (over z, x), items: 8 (over y, core).
Axes of the slice: x: 4, y: 4, z: 4, core: 2. Of those that a mesh axis runs over, the one named last changes fastest.
Arguments:
- interactions: bfloat16 [32768, 32768], P('users', 'items'), may hold values from 0 to 13, as said below
- user_weights: bfloat16 [32768], P('users'), may hold values from 0.3 to 9, as said below
- panel_index: int32 [1], replicated, may hold values from 0 to 127
Outputs:
- item_covariance: float32 [8, 4096, 256], P(None, ('users', 'items'))
- item_mean: float32 [8, 4096], P(None, ('users', 'items'))
The draws below stay inside these ranges and needn't reach their ends.
Inputs may be any that keep to these rules, and one draw needn't show every extreme that they name: `user_weights`: positive user weights. `interactions`: confidences are zero or positive.
All inputs are finite; a program needn't handle non-finite values.
Results may differ from the reference program's by a relative error of at most 0.00031.
Values may be sent and summed in bfloat16 or wider, within the bound.
No kernel may reach another device: no remote copies, remote signals or barrier semaphores. Data moves between devices by JAX's collectives and lax.ppermute only.
A program may use at most 384 MiB of HBM per device.

```python
import jax
import jax.numpy as jnp
from jax import lax

N = 32768
P_SIZE = 256
BLK = 32
USR_DEV = 2048
USERS = 32768
CYC = 8
N_USERS = 16
N_ITEMS = 8


def draw_interactions(key, part):
    key = jax.random.fold_in(key, 11)
    keys = jax.random.split(key, 4)
    activity = jnp.clip(0.7 * jax.random.normal(keys[0], (USERS, 1), jnp.float32), -2.1, 2.1)
    spread = jax.random.uniform(keys[1], (USERS, N), jnp.float32, 0.5, 1.5)
    popular = jax.random.uniform(keys[2], (1, N), jnp.float32, 0.3, 0.8)
    chance = jax.random.uniform(keys[3], (USERS, N), jnp.float32)
    present = jnp.where(chance < popular, 1.0, 0.0)
    return (present * jnp.exp(activity) * spread).astype(jnp.bfloat16)


def draw_user_weights(key, part):
    key = jax.random.fold_in(key, 23)
    base = jnp.exp(jax.random.uniform(key, (USERS,), jnp.float32, jnp.log(0.3), jnp.log(3.0)))
    ramp = 1.0 + 2.0 * jnp.arange(USERS, dtype=jnp.float32) / (USERS - 1)
    return (base * ramp).astype(jnp.bfloat16)


def setup_inputs(seed: int = 0) -> dict:
    key_list = jax.random.split(jax.random.key(seed), 4)
    return {
        "interactions": draw_interactions(jax.random.fold_in(key_list[3], 71), 0),
        "user_weights": draw_user_weights(jax.random.fold_in(key_list[3], 71), 0),
        "panel_index": jax.random.randint(key_list[2], (1,), 0, N // P_SIZE).astype(jnp.int32),
    }


def reference(interactions, user_weights, panel_index):
    start = panel_index[0].astype(jnp.int32) * P_SIZE
    panel = lax.dynamic_slice_in_dim(interactions, start, P_SIZE, 1)
    weights32 = user_weights.astype(jnp.float32)
    weighted = (weights32[:, None] * panel.astype(jnp.float32)).astype(jnp.bfloat16)
    blocks = interactions.reshape(N_USERS, USR_DEV, N)
    weighted_blocks = weighted.reshape(N_USERS, USR_DEV, P_SIZE)
    weight_blocks = user_weights.reshape(N_USERS, USR_DEV)

    def accumulate(carry, pieces):
        gram, colsum = carry
        block, wpanel, wrow = pieces
        dense = block.astype(jnp.float32)
        gram = gram + jnp.dot(dense.T, wpanel.astype(jnp.float32))
        colsum = colsum + jnp.dot(wrow.astype(jnp.float32), dense)
        return (gram, colsum), None

    start_carry = (jnp.zeros((N, P_SIZE), jnp.float32), jnp.zeros((N,), jnp.float32))
    (gram, colsum), _ = lax.scan(accumulate, start_carry, (blocks, weighted_blocks, weight_blocks))
    count = jnp.sum(weights32)
    panel_sum = jnp.dot(weights32, panel.astype(jnp.float32))
    mean = colsum / count
    panel_mean = panel_sum / count
    covariance = gram / count - mean[:, None] * panel_mean[None, :]
    width = BLK * N_USERS * N_ITEMS
    return covariance.reshape(CYC, width, P_SIZE), mean.reshape(CYC, width)
```

```python
import functools

import jax
import jax.numpy as jnp
from jax import lax
from jax.experimental import pallas as pl
from jax.experimental.pallas import tpu as pltpu
from jax.sharding import PartitionSpec as P

P_SIZE = 256
BLK = 32
LANES = 128
CORES = 2
EXTRA = 8
F32 = jnp.float32
BF16 = jnp.bfloat16


def split3(value):
    parts = []
    for _ in range(3):
        part = value.astype(BF16).astype(F32)
        parts.append(part)
        value = value - part
    return parts


def moment_kernel(tile, x_ref, panel_ref, wcol_ref, wrow_ref, out_ref, lhs, pcol, fixed):
    users = x_ref.shape[0]
    step = users // 4

    @pl.when(pl.program_id(0) == 0)
    def _():
        for r in range(0, users, step):
            rows = pl.ds(r, step)
            weighted = (wcol_ref[rows, :] * panel_ref[rows, :].astype(F32)).astype(BF16)
            lhs[0:P_SIZE, r : r + step] = weighted.T
        wrow = wrow_ref[...]
        lhs[P_SIZE:, :] = jnp.broadcast_to(wrow, (16, users))
        count = jnp.sum(wrow.astype(F32), axis=1, keepdims=True)
        total = jnp.dot(
            jnp.broadcast_to(wrow, (8, users)), panel_ref[...], preferred_element_type=F32
        )
        mean = total / count
        pcol[...] = jnp.concatenate([mean] * 16, axis=0).T
        hi, mid, lo = split3(mean[0:1])
        chi, cmid, clo = split3(jnp.broadcast_to(count, (1, LANES)))
        rows = [v[:, h : h + LANES] for v in (hi, mid, lo) for h in (0, LANES)]
        lane = lax.broadcasted_iota(jnp.int32, (1, LANES), 1)
        last = jnp.where(lane < 32, chi, jnp.where(lane < 64, cmid, clo))
        fixed[...] = jnp.concatenate(rows + [jnp.broadcast_to(count, (1, LANES)), last], axis=0)

    acc = jnp.dot(lhs[...], x_ref[...], preferred_element_type=F32)
    inverse = 1.0 / fixed[6:7, 0:1]
    mrow = acc[P_SIZE : P_SIZE + 1, :] * inverse
    moment = acc[0:P_SIZE, :] * inverse - pcol[:, 0:1] * mrow
    top = jnp.max(jnp.max(jnp.abs(moment), axis=0, keepdims=True), axis=1, keepdims=True)
    scale = (32768.0 / jnp.maximum(top, 1e-30)).astype(BF16).astype(F32)
    v = moment * scale
    v2 = v * v
    coded = (v * jnp.abs(v) * v2 * (v2 * v2)).astype(BF16).T
    pieces = tile // BLK
    coded = coded.reshape(pieces, BLK, P_SIZE)
    out_ref[:, 0:BLK, :] = coded[:, :, 0:LANES]
    out_ref[:, BLK : 2 * BLK, :] = coded[:, :, LANES:]

    hi, mid, lo = split3(mrow)
    lane = lax.broadcasted_iota(jnp.int32, (1, tile), 1) % LANES
    lane8 = lax.broadcasted_iota(jnp.int32, (EXTRA, LANES), 1)
    row8 = lax.broadcasted_iota(jnp.int32, (EXTRA, LANES), 0)
    base = jnp.where((row8 == 7) & (lane8 >= 96), scale, fixed[...])
    per = LANES // BLK
    for q in range(per):
        mix = jnp.where(
            lane < 32,
            pltpu.roll(hi, (tile - 32 * q) % tile, 1),
            jnp.where(
                lane < 64,
                pltpu.roll(mid, (tile + 32 - 32 * q) % tile, 1),
                pltpu.roll(lo, (tile + 64 - 32 * q) % tile, 1),
            ),
        )
        for g in range(tile // LANES):
            row = jnp.broadcast_to(mix[:, g * LANES : (g + 1) * LANES], (EXTRA, LANES))
            stats = jnp.where(row8 == 6, row, base).astype(BF16)
            out_ref[g * per + q, 2 * BLK :, :] = stats


def moments(x, panel, weights, pieces):
    users, items = x.shape
    tile = 512
    return pl.pallas_call(
        functools.partial(moment_kernel, tile),
        grid=(items // tile,),
        in_specs=[
            pl.BlockSpec((users, tile), lambda i: (0, i)),
            pl.BlockSpec((users, P_SIZE), lambda i: (0, 0)),
            pl.BlockSpec((users, 1), lambda i: (0, 0)),
            pl.BlockSpec((1, users), lambda i: (0, 0)),
        ],
        out_specs=pl.BlockSpec((tile // BLK, 2 * BLK + EXTRA, LANES), lambda i: (i, 0, 0)),
        out_shape=jax.ShapeDtypeStruct((pieces, 2 * BLK + EXTRA, LANES), BF16),
        scratch_shapes=[
            pltpu.VMEM((P_SIZE + 16, users), BF16),
            pltpu.VMEM((P_SIZE, LANES), F32),
            pltpu.VMEM((EXTRA, LANES), F32),
        ],
        compiler_params=pltpu.CompilerParams(
            vmem_limit_bytes=40 * 2**20, dimension_semantics=("arbitrary",)
        ),
        cost_estimate=pl.CostEstimate(
            flops=2 * users * items * P_SIZE, bytes_accessed=20 * 2**20, transcendentals=0
        ),
    )(x, panel, weights.astype(F32).reshape(-1, 1), weights.reshape(1, -1))


def merge_kernel(groups, cycles, in_ref, cov_ref, mean_ref):
    stats0 = in_ref[:, 0, 2 * BLK :, :].astype(F32)
    part = lambda row: jnp.concatenate([stats0[:, row, :], stats0[:, row + 1, :]], axis=1)
    panel = part(0) + part(2) + part(4)
    last = stats0[:, 7, :]
    count = last[:, 0:1] + last[:, 32:33] + last[:, 64:65]
    share = count / jnp.sum(count, axis=0, keepdims=True)
    panel_dev = panel - jnp.sum(share * panel, axis=0, keepdims=True)
    for i in range(cycles):
        stats = in_ref[:, i, 2 * BLK :, :].astype(F32)
        row = stats[:, 6, :]
        mean = row[:, 0:32] + row[:, 32:64] + row[:, 64:96]
        mean_all = jnp.sum(share * mean, axis=0, keepdims=True)
        mean_ref[i : i + 1, :] = mean_all
        left = jnp.broadcast_to(share, (groups, 32)) * (mean - mean_all)
        left = jnp.concatenate([left] * 4, axis=1).T
        back = share / stats[:, 7, 96:97]
        first = jnp.zeros((BLK, LANES), F32)
        second = jnp.zeros((BLK, LANES), F32)
        for u in range(groups):
            y = in_ref[u, i, 0 : 2 * BLK, :].astype(F32)
            size = jnp.exp2(jnp.log2(jnp.abs(y)) * 0.125)
            v = jnp.where(y < 0, -size, size) * back[u : u + 1, :]
            col = left[0:BLK, u : u + 1]
            first = first + v[0:BLK] + col * panel_dev[u : u + 1, 0:LANES]
            second = second + v[BLK:] + col * panel_dev[u : u + 1, LANES:]
        cov_ref[i, :, 0:LANES] = first
        cov_ref[i, :, LANES:] = second


def merge(pieces, groups, cycles):
    return pl.pallas_call(
        functools.partial(merge_kernel, groups, cycles),
        out_shape=[
            jax.ShapeDtypeStruct((cycles, BLK, P_SIZE), F32),
            jax.ShapeDtypeStruct((cycles, BLK), F32),
        ],
        in_specs=[pl.BlockSpec(memory_space=pltpu.VMEM)],
        out_specs=[pl.BlockSpec(memory_space=pltpu.VMEM)] * 2,
        compiler_params=pltpu.CompilerParams(vmem_limit_bytes=24 * 2**20),
        cost_estimate=pl.CostEstimate(
            flops=20 * 2**20, bytes_accessed=3 * 2**20, transcendentals=2 * 2**20
        ),
    )(pieces.reshape(groups, cycles, *pieces.shape[1:]))


def spread_panel(x, chosen):
    users, items = x.shape
    ring = lax.axis_size("items")
    chips = ring // CORES
    me = lax.axis_index("items")
    core, chip = me % CORES, me // CORES
    owner = chosen // (items // P_SIZE)
    start = chosen % (items // P_SIZE) * P_SIZE
    half = users // CORES
    own = lax.dynamic_slice(x, (core * half, start), (half, P_SIZE))
    other = lax.dynamic_slice(x, ((1 - core) * half, start), (half, P_SIZE))
    across = [(i, i ^ 1) for i in range(ring)]
    got = lax.ppermute(other, "items", across)
    mine = jnp.where(core == owner % CORES, own, got)

    def send_from(root):
        def branch(block):
            return tuple(
                lax.ppermute(
                    block,
                    "items",
                    [
                        (root * CORES + c, (root + d) % chips * CORES + c)
                        for c in range(CORES)
                    ],
                )
                for d in range(1, chips)
            )

        return branch

    moved = lax.switch(owner // CORES, [send_from(root) for root in range(chips)], mine)
    away = (chip - owner // CORES) % chips
    for d, block in enumerate(moved):
        mine = jnp.where(away == d + 1, block, mine)
    got = lax.ppermute(mine, "items", across)
    low = jnp.where(core == 0, mine, got)
    high = jnp.where(core == 0, got, mine)
    return jnp.concatenate([low, high], axis=0)


def per_device(interactions, user_weights, panel_index):
    groups, ring = lax.axis_size("users"), lax.axis_size("items")
    panel = spread_panel(interactions, panel_index[0])
    pieces = moments(interactions, panel, user_weights, groups * ring)
    moved = lax.all_to_all(pieces, ("users", "items"), 0, 0, tiled=True)
    return tuple(merge(moved, groups, ring))


def solution(mesh):
    return jax.shard_map(
        per_device,
        mesh=mesh,
        in_specs=(P("users", "items"), P("users"), P()),
        out_specs=(P(None, ("users", "items"), None), P(None, ("users", "items"))),
        check_vma=False,
    )
```

```python
import functools

import jax
import jax.numpy as jnp
from jax import lax
from jax.experimental import pallas as pl
from jax.experimental.pallas import tpu as pltpu
from jax.sharding import PartitionSpec as P

P_SIZE = 256
BLK = 32
LANES = 128
CORES = 2
CORE, AWAY, SAME = range(3)
EXTRA = 8
F32 = jnp.float32
BF16 = jnp.bfloat16


def split3(value):
    parts = []
    for _ in range(3):
        part = value.astype(BF16).astype(F32)
        parts.append(part)
        value = value - part
    return parts


def touch_kernel(x_ref, after_ref, out_ref):
    out_ref[...] = jnp.zeros_like(out_ref)


def touch(x, after):
    return pl.pallas_call(
        touch_kernel,
        in_specs=[pl.BlockSpec(memory_space=pltpu.VMEM), pl.BlockSpec(memory_space=pl.ANY)],
        out_specs=pl.BlockSpec(memory_space=pltpu.VMEM),
        out_shape=jax.ShapeDtypeStruct((8, LANES), F32),
        compiler_params=pltpu.CompilerParams(vmem_limit_bytes=2 * 2**20),
        cost_estimate=pl.CostEstimate(
            flops=0, bytes_accessed=x.size * x.dtype.itemsize, transcendentals=0
        ),
    )(x, after)


def turn_kernel(right_ref, left_ref, after_ref, first_ref, second_ref):
    part = first_ref.shape[0]
    first_ref[...] = right_ref[0:part, :]
    second_ref[...] = left_ref[part:, :]


def turn(right, left, after):
    rows, columns = right.shape
    shape = jax.ShapeDtypeStruct((rows // 2, columns), right.dtype)
    return pl.pallas_call(
        turn_kernel,
        in_specs=[pl.BlockSpec(memory_space=pltpu.VMEM)] * 2 + [pl.BlockSpec(memory_space=pl.ANY)],
        out_specs=[pl.BlockSpec(memory_space=pltpu.VMEM)] * 2,
        out_shape=[shape, shape],
        compiler_params=pltpu.CompilerParams(vmem_limit_bytes=4 * 2**20),
        cost_estimate=pl.CostEstimate(flops=0, bytes_accessed=2**20, transcendentals=0),
    )(right, left, after)


def choose_kernel(info_ref, own_ref, got_ref, out_ref):
    @pl.when(info_ref[SAME] == 1)
    def _():
        out_ref[...] = own_ref[...]

    @pl.when(info_ref[SAME] != 1)
    def _():
        out_ref[...] = got_ref[...]


def join_kernel(info_ref, mine_ref, right_ref, left_ref, far_a_ref, far_b_ref, out_ref):
    part = far_a_ref.shape[0]
    for k, ref in ((0, mine_ref), (1, right_ref), (3, left_ref)):

        @pl.when(info_ref[AWAY] == k)
        def _():
            out_ref[...] = ref[...]

    @pl.when(info_ref[AWAY] == 2)
    def _():
        out_ref[0:part, :] = far_a_ref[...]
        out_ref[part:, :] = far_b_ref[...]


def select(kernel, info, *blocks):
    return pl.pallas_call(
        kernel,
        in_specs=[pl.BlockSpec(memory_space=pltpu.SMEM)]
        + [pl.BlockSpec(memory_space=pltpu.VMEM)] * len(blocks),
        out_specs=pl.BlockSpec(memory_space=pltpu.VMEM),
        out_shape=jax.ShapeDtypeStruct(blocks[0].shape, blocks[0].dtype),
        compiler_params=pltpu.CompilerParams(vmem_limit_bytes=2 * 2**20),
        cost_estimate=pl.CostEstimate(flops=0, bytes_accessed=2**20, transcendentals=0),
    )(info, *blocks)


def moment_kernel(tile, info_ref, w_ref, mine_ref, other_ref, x_ref, out_ref, lhs):
    users, items = x_ref.shape
    half = users // CORES
    lanes16 = w_ref[...]
    wrow = jnp.concatenate([lanes16[k : k + 1, :] for k in range(users // LANES)], axis=1)
    wrow32 = wrow.astype(F32)
    count = jnp.sum(wrow32, axis=1, keepdims=True)
    total = jnp.zeros((P_SIZE, LANES), F32)
    first = info_ref[CORE] == 0
    low = jnp.where(first, mine_ref[...], other_ref[...])
    high = jnp.where(first, other_ref[...], mine_ref[...])
    for k, part in enumerate((low, high)):
        cut = slice(k * half, (k + 1) * half)
        product = part.T.astype(F32) * wrow32[:, cut]
        lhs[0:P_SIZE, cut] = product.astype(BF16)
        for g in range(0, half, LANES):
            total += product[:, g : g + LANES]
    lhs[P_SIZE:, :] = jnp.broadcast_to(wrow, (16, users))
    inverse = 1.0 / count
    pcol = jnp.sum(total, axis=1, keepdims=True) * inverse
    prow = jnp.broadcast_to(pcol, (P_SIZE, LANES)).T[0:1, :]
    hi, mid, lo = split3(prow)
    chi, cmid, clo = split3(jnp.broadcast_to(count, (1, LANES)))
    rows = [v[:, h : h + LANES] for v in (hi, mid, lo) for h in (0, LANES)]
    lane1 = lax.broadcasted_iota(jnp.int32, (1, LANES), 1)
    last = jnp.where(lane1 < 32, chi, jnp.where(lane1 < 64, cmid, clo))
    fixed = jnp.concatenate(rows + [last, last], axis=0)
    lane = lax.broadcasted_iota(jnp.int32, (1, tile), 1) % LANES
    lane8 = lax.broadcasted_iota(jnp.int32, (EXTRA, LANES), 1)
    row8 = lax.broadcasted_iota(jnp.int32, (EXTRA, LANES), 0)
    per = LANES // BLK
    pieces = tile // BLK

    for t in range(items // tile):
        acc = jnp.dot(
            lhs[...], x_ref[:, t * tile : (t + 1) * tile], preferred_element_type=F32
        )
        mrow = acc[P_SIZE : P_SIZE + 1, :] * inverse
        moment = acc[0:P_SIZE, :] * inverse - pcol * mrow
        top = jnp.max(jnp.max(jnp.abs(moment), axis=0, keepdims=True), axis=1, keepdims=True)
        scale = (32768.0 / jnp.maximum(top, 1e-30)).astype(BF16).astype(F32)
        v = moment * scale
        v2 = v * v
        coded = (v * jnp.abs(v) * v2 * (v2 * v2)).astype(BF16).T.reshape(pieces, BLK, P_SIZE)
        place = slice(t * pieces, (t + 1) * pieces)
        out_ref[place, 0:BLK, :] = coded[:, :, 0:LANES]
        out_ref[place, BLK : 2 * BLK, :] = coded[:, :, LANES:]
        hi, mid, lo = split3(mrow)
        base = jnp.where((row8 == 7) & (lane8 >= 96), scale, fixed)
        for q in range(per):
            mix = jnp.where(
                lane < 32,
                pltpu.roll(hi, (tile - 32 * q) % tile, 1),
                jnp.where(
                    lane < 64,
                    pltpu.roll(mid, (tile + 32 - 32 * q) % tile, 1),
                    pltpu.roll(lo, (tile + 64 - 32 * q) % tile, 1),
                ),
            )
            for g in range(tile // LANES):
                row = jnp.broadcast_to(mix[:, g * LANES : (g + 1) * LANES], (EXTRA, LANES))
                stats = jnp.where(row8 == 6, row, base).astype(BF16)
                out_ref[t * pieces + g * per + q, 2 * BLK :, :] = stats


def moments(info, x, mine, other, weights, pieces):
    users, items = x.shape
    tile = 512
    return pl.pallas_call(
        functools.partial(moment_kernel, tile),
        in_specs=[pl.BlockSpec(memory_space=pltpu.SMEM)]
        + [pl.BlockSpec(memory_space=pltpu.VMEM)] * 4,
        out_specs=pl.BlockSpec(memory_space=pltpu.VMEM),
        out_shape=jax.ShapeDtypeStruct((pieces, 2 * BLK + EXTRA, LANES), BF16),
        scratch_shapes=[pltpu.VMEM((P_SIZE + 16, users), BF16)],
        compiler_params=pltpu.CompilerParams(vmem_limit_bytes=16 * 2**20),
        cost_estimate=pl.CostEstimate(
            flops=2 * users * items * P_SIZE, bytes_accessed=4 * 2**20, transcendentals=0
        ),
    )(info, weights.reshape(-1, LANES), mine, other, x)


def merge_kernel(groups, cycles, in_ref, cov_ref, mean_ref):
    stats0 = in_ref[:, 0, 2 * BLK :, :].astype(F32)
    part = lambda row: jnp.concatenate([stats0[:, row, :], stats0[:, row + 1, :]], axis=1)
    panel = part(0) + part(2) + part(4)
    last = stats0[:, 7, :]
    count = last[:, 0:1] + last[:, 32:33] + last[:, 64:65]
    share = count / jnp.sum(count, axis=0, keepdims=True)
    panel_dev = panel - jnp.sum(share * panel, axis=0, keepdims=True)
    for i in range(cycles):
        stats = in_ref[:, i, 2 * BLK :, :].astype(F32)
        row = stats[:, 6, :]
        mean = row[:, 0:32] + row[:, 32:64] + row[:, 64:96]
        mean_all = jnp.sum(share * mean, axis=0, keepdims=True)
        mean_ref[i : i + 1, :] = mean_all
        left = jnp.broadcast_to(share, (groups, 32)) * (mean - mean_all)
        left = jnp.concatenate([left] * 4, axis=1).T
        back = share / stats[:, 7, 96:97]
        first = jnp.zeros((BLK, LANES), F32)
        second = jnp.zeros((BLK, LANES), F32)
        for u in range(groups):
            y = in_ref[u, i, 0 : 2 * BLK, :].astype(F32)
            size = jnp.exp2(jnp.log2(jnp.abs(y)) * 0.125)
            v = jnp.where(y < 0, -size, size) * back[u : u + 1, :]
            col = left[0:BLK, u : u + 1]
            first = first + v[0:BLK] + col * panel_dev[u : u + 1, 0:LANES]
            second = second + v[BLK:] + col * panel_dev[u : u + 1, LANES:]
        cov_ref[i, :, 0:LANES] = first
        cov_ref[i, :, LANES:] = second


def merge(pieces, groups, cycles):
    return pl.pallas_call(
        functools.partial(merge_kernel, groups, cycles),
        out_shape=[
            jax.ShapeDtypeStruct((cycles, BLK, P_SIZE), F32),
            jax.ShapeDtypeStruct((cycles, BLK), F32),
        ],
        in_specs=[pl.BlockSpec(memory_space=pltpu.VMEM)],
        out_specs=[pl.BlockSpec(memory_space=pltpu.VMEM)] * 2,
        compiler_params=pltpu.CompilerParams(vmem_limit_bytes=24 * 2**20),
        cost_estimate=pl.CostEstimate(
            flops=20 * 2**20, bytes_accessed=3 * 2**20, transcendentals=2 * 2**20
        ),
    )(pieces.reshape(groups, cycles, *pieces.shape[1:]))


def spread_panel(x, info, core, start):
    ring = lax.axis_size("items")
    chips = ring // CORES
    half = x.shape[0] // CORES
    across = [(i, i ^ 1) for i in range(ring)]

    def step(block, distance):
        pairs = [
            (y * CORES + c, (y + distance) % chips * CORES + c)
            for y in range(chips)
            for c in range(CORES)
        ]
        return lax.ppermute(block, "items", pairs)

    own = lax.dynamic_slice(x, (core * half, start), (half, P_SIZE))
    other = lax.dynamic_slice(x, ((1 - core) * half, start), (half, P_SIZE))
    mine = select(choose_kernel, info, own, lax.ppermute(other, "items", across))
    right, left = step(mine, 1), step(mine, -1)
    first, second = turn(right, left, touch(x, mine))
    far_a, far_b = step(first, 1), step(second, -1)
    mine = select(join_kernel, info, mine, right, left, far_a, far_b)
    return mine, lax.ppermute(mine, "items", across)


def per_device(interactions, user_weights, panel_index):
    groups, ring = lax.axis_size("users"), lax.axis_size("items")
    me, chips = lax.axis_index("items"), ring // CORES
    per_shard = interactions.shape[1] // P_SIZE
    owner, place = panel_index[0] // per_shard, panel_index[0] % per_shard
    core = me % CORES
    away = (me // CORES - owner // CORES) % chips
    same = (core == owner % CORES).astype(jnp.int32)
    info = jnp.stack([core, away, same]).astype(jnp.int32)
    mine, other = spread_panel(interactions, info, core, place * P_SIZE)
    pieces = moments(info, interactions, mine, other, user_weights, groups * ring)
    moved = lax.all_to_all(pieces, ("users", "items"), 0, 0, tiled=True)
    return tuple(merge(moved, groups, ring))


def solution(mesh):
    return jax.shard_map(
        per_device,
        mesh=mesh,
        in_specs=(P("users", "items"), P("users"), P()),
        out_specs=(P(None, ("users", "items"), None), P(None, ("users", "items"))),
        check_vma=False,
    )
```

```python
import functools

import jax
import jax.numpy as jnp
from jax import lax
from jax.experimental import pallas as pl
from jax.experimental.pallas import tpu as pltpu
from jax.sharding import PartitionSpec as P

P_SIZE = 256
BLK = 32
LANES = 128
CORES = 2
CORE, AWAY, SAME = range(3)
EXTRA = 8
F32 = jnp.float32
BF16 = jnp.bfloat16


def split3(value):
    parts = []
    for _ in range(3):
        part = value.astype(BF16).astype(F32)
        parts.append(part)
        value = value - part
    return parts


def touch_kernel(x_ref, after_ref, out_ref):
    out_ref[...] = jnp.zeros_like(out_ref)


def touch(x, after):
    return pl.pallas_call(
        touch_kernel,
        in_specs=[pl.BlockSpec(memory_space=pltpu.VMEM), pl.BlockSpec(memory_space=pl.ANY)],
        out_specs=pl.BlockSpec(memory_space=pltpu.VMEM),
        out_shape=jax.ShapeDtypeStruct((8, LANES), F32),
        compiler_params=pltpu.CompilerParams(vmem_limit_bytes=2 * 2**20),
        cost_estimate=pl.CostEstimate(
            flops=0, bytes_accessed=x.size * x.dtype.itemsize, transcendentals=0
        ),
    )(x, after)


def turn_kernel(right_ref, left_ref, after_ref, first_ref, second_ref):
    part = first_ref.shape[0]
    first_ref[...] = right_ref[0:part, :]
    second_ref[...] = left_ref[part:, :]


def turn(right, left, after):
    rows, columns = right.shape
    shape = jax.ShapeDtypeStruct((rows // 2, columns), right.dtype)
    return pl.pallas_call(
        turn_kernel,
        in_specs=[pl.BlockSpec(memory_space=pltpu.VMEM)] * 2 + [pl.BlockSpec(memory_space=pl.ANY)],
        out_specs=[pl.BlockSpec(memory_space=pltpu.VMEM)] * 2,
        out_shape=[shape, shape],
        compiler_params=pltpu.CompilerParams(vmem_limit_bytes=4 * 2**20),
        cost_estimate=pl.CostEstimate(flops=0, bytes_accessed=2**20, transcendentals=0),
    )(right, left, after)


def choose_kernel(info_ref, own_ref, got_ref, out_ref):
    @pl.when(info_ref[SAME] == 1)
    def _():
        out_ref[...] = own_ref[...]

    @pl.when(info_ref[SAME] != 1)
    def _():
        out_ref[...] = got_ref[...]


def join_kernel(info_ref, mine_ref, right_ref, left_ref, far_a_ref, far_b_ref, out_ref):
    part = far_a_ref.shape[0]
    for k, ref in ((0, mine_ref), (1, right_ref), (3, left_ref)):

        @pl.when(info_ref[AWAY] == k)
        def _():
            out_ref[...] = ref[...]

    @pl.when(info_ref[AWAY] == 2)
    def _():
        out_ref[0:part, :] = far_a_ref[...]
        out_ref[part:, :] = far_b_ref[...]


def select(kernel, info, *blocks):
    return pl.pallas_call(
        kernel,
        in_specs=[pl.BlockSpec(memory_space=pltpu.SMEM)]
        + [pl.BlockSpec(memory_space=pltpu.VMEM)] * len(blocks),
        out_specs=pl.BlockSpec(memory_space=pltpu.VMEM),
        out_shape=jax.ShapeDtypeStruct(blocks[0].shape, blocks[0].dtype),
        compiler_params=pltpu.CompilerParams(vmem_limit_bytes=2 * 2**20),
        cost_estimate=pl.CostEstimate(flops=0, bytes_accessed=2**20, transcendentals=0),
    )(info, *blocks)


def left_side(core, w_ref, block_ref, lhs):
    half = block_ref.shape[0]
    lanes16 = w_ref[...].astype(F32)
    per = half // LANES
    rows = jnp.where(core == 0, lanes16[0:per], lanes16[per:])
    wrow = jnp.concatenate([rows[k : k + 1, :] for k in range(per)], axis=1)
    product = block_ref[...].T.astype(F32) * wrow
    lhs[0:P_SIZE, :] = product.astype(BF16)
    lhs[P_SIZE:, :] = jnp.broadcast_to(wrow, (16, half)).astype(BF16)
    total = product[:, 0:LANES]
    for g in range(LANES, half, LANES):
        total += product[:, g : g + LANES]
    return total


def own_kernel(tile, info_ref, w_ref, block_ref, x_ref, acc_ref, total_ref, lhs):
    half, core = block_ref.shape[0], info_ref[CORE]
    total_ref[...] = left_side(core, w_ref, block_ref, lhs)
    users = pl.ds(pl.multiple_of(core * half, half), half)
    for t in range(x_ref.shape[1] // tile):
        cut = slice(t * tile, (t + 1) * tile)
        acc_ref[:, cut] = jnp.dot(lhs[...], x_ref[users, cut], preferred_element_type=F32)


def own_half(info, x, block, weights):
    users, items = x.shape
    return pl.pallas_call(
        functools.partial(own_kernel, 512),
        in_specs=[pl.BlockSpec(memory_space=pltpu.SMEM)]
        + [pl.BlockSpec(memory_space=pltpu.VMEM)] * 3,
        out_specs=[pl.BlockSpec(memory_space=pltpu.VMEM)] * 2,
        out_shape=[
            jax.ShapeDtypeStruct((P_SIZE + 16, items), F32),
            jax.ShapeDtypeStruct((P_SIZE, LANES), F32),
        ],
        scratch_shapes=[pltpu.VMEM((P_SIZE + 16, users // CORES), BF16)],
        compiler_params=pltpu.CompilerParams(vmem_limit_bytes=12 * 2**20),
        cost_estimate=pl.CostEstimate(
            flops=users * items * P_SIZE, bytes_accessed=4 * 2**20, transcendentals=0
        ),
    )(info, weights.reshape(-1, LANES), block, x)


def moment_kernel(
    tile, info_ref, w_ref, block_ref, x_ref, acc_ref, total_ref, out_ref, lhs
):
    items = x_ref.shape[1]
    half, core = block_ref.shape[0], 1 - info_ref[CORE]
    total = total_ref[...] + left_side(core, w_ref, block_ref, lhs)
    users = pl.ds(pl.multiple_of(core * half, half), half)
    weights = w_ref[...].astype(F32)
    count = jnp.sum(jnp.sum(weights, axis=0, keepdims=True), axis=1, keepdims=True)
    inverse = 1.0 / count
    pcol = jnp.sum(total, axis=1, keepdims=True) * inverse
    prow = jnp.broadcast_to(pcol, (P_SIZE, LANES)).T[0:1, :]
    hi, mid, lo = split3(prow)
    chi, cmid, clo = split3(jnp.broadcast_to(count, (1, LANES)))
    rows = [v[:, h : h + LANES] for v in (hi, mid, lo) for h in (0, LANES)]
    lane1 = lax.broadcasted_iota(jnp.int32, (1, LANES), 1)
    last = jnp.where(lane1 < 32, chi, jnp.where(lane1 < 64, cmid, clo))
    fixed = jnp.concatenate(rows + [last, last], axis=0)
    lane = lax.broadcasted_iota(jnp.int32, (1, tile), 1) % LANES
    lane8 = lax.broadcasted_iota(jnp.int32, (EXTRA, LANES), 1)
    row8 = lax.broadcasted_iota(jnp.int32, (EXTRA, LANES), 0)
    per = LANES // BLK
    pieces = tile // BLK

    for t in range(items // tile):
        cut = slice(t * tile, (t + 1) * tile)
        acc = acc_ref[:, cut] + jnp.dot(
            lhs[...], x_ref[users, cut], preferred_element_type=F32
        )
        mrow = acc[P_SIZE : P_SIZE + 1, :] * inverse
        moment = acc[0:P_SIZE, :] * inverse - pcol * mrow
        top = jnp.max(jnp.max(jnp.abs(moment), axis=0, keepdims=True), axis=1, keepdims=True)
        scale = (32768.0 / jnp.maximum(top, 1e-30)).astype(BF16).astype(F32)
        v = moment * scale
        v2 = v * v
        coded = (v * jnp.abs(v) * v2 * (v2 * v2)).astype(BF16).T.reshape(pieces, BLK, P_SIZE)
        place = slice(t * pieces, (t + 1) * pieces)
        out_ref[place, 0:BLK, :] = coded[:, :, 0:LANES]
        out_ref[place, BLK : 2 * BLK, :] = coded[:, :, LANES:]
        hi, mid, lo = split3(mrow)
        base = jnp.where((row8 == 7) & (lane8 >= 96), scale, fixed)
        for q in range(per):
            mix = jnp.where(
                lane < 32,
                pltpu.roll(hi, (tile - 32 * q) % tile, 1),
                jnp.where(
                    lane < 64,
                    pltpu.roll(mid, (tile + 32 - 32 * q) % tile, 1),
                    pltpu.roll(lo, (tile + 64 - 32 * q) % tile, 1),
                ),
            )
            for g in range(tile // LANES):
                row = jnp.broadcast_to(mix[:, g * LANES : (g + 1) * LANES], (EXTRA, LANES))
                stats = jnp.where(row8 == 6, row, base).astype(BF16)
                out_ref[t * pieces + g * per + q, 2 * BLK :, :] = stats


def moments(info, x, mine, other, weights, pieces):
    acc, total = own_half(info, x, mine, weights)
    users, items = x.shape
    tile = 512
    return pl.pallas_call(
        functools.partial(moment_kernel, tile),
        in_specs=[pl.BlockSpec(memory_space=pltpu.SMEM)]
        + [pl.BlockSpec(memory_space=pltpu.VMEM)] * 5,
        out_specs=pl.BlockSpec(memory_space=pltpu.VMEM),
        out_shape=jax.ShapeDtypeStruct((pieces, 2 * BLK + EXTRA, LANES), BF16),
        scratch_shapes=[pltpu.VMEM((P_SIZE + 16, users // CORES), BF16)],
        compiler_params=pltpu.CompilerParams(vmem_limit_bytes=16 * 2**20),
        cost_estimate=pl.CostEstimate(
            flops=users * items * P_SIZE, bytes_accessed=4 * 2**20, transcendentals=0
        ),
    )(info, weights.reshape(-1, LANES), other, x, acc, total)


def merge_kernel(groups, cycles, in_ref, cov_ref, mean_ref):
    stats0 = in_ref[:, 0, 2 * BLK :, :].astype(F32)
    part = lambda row: jnp.concatenate([stats0[:, row, :], stats0[:, row + 1, :]], axis=1)
    panel = part(0) + part(2) + part(4)
    last = stats0[:, 7, :]
    count = last[:, 0:1] + last[:, 32:33] + last[:, 64:65]
    share = count / jnp.sum(count, axis=0, keepdims=True)
    panel_dev = panel - jnp.sum(share * panel, axis=0, keepdims=True)
    for i in range(cycles):
        stats = in_ref[:, i, 2 * BLK :, :].astype(F32)
        row = stats[:, 6, :]
        mean = row[:, 0:32] + row[:, 32:64] + row[:, 64:96]
        mean_all = jnp.sum(share * mean, axis=0, keepdims=True)
        mean_ref[i : i + 1, :] = mean_all
        left = jnp.broadcast_to(share, (groups, 32)) * (mean - mean_all)
        between = lax.dot_general(
            left,
            panel_dev,
            (((0,), (0,)), ((), ())),
            precision=lax.Precision.HIGHEST,
            preferred_element_type=F32,
        )
        back = share / stats[:, 7, 96:97]
        within = jnp.zeros((2 * BLK, LANES), F32)
        for u in range(groups):
            y = in_ref[u, i, 0 : 2 * BLK, :].astype(F32)
            shrink = jnp.exp2(-0.875 * jnp.log2(jnp.maximum(jnp.abs(y), 1e-37)))
            within = within + (y * back[u : u + 1, :]) * shrink
        first = within[0:BLK] + between[:, 0:LANES]
        second = within[BLK:] + between[:, LANES:]
        cov_ref[i, :, 0:LANES] = first
        cov_ref[i, :, LANES:] = second


def merge(pieces, groups, cycles):
    return pl.pallas_call(
        functools.partial(merge_kernel, groups, cycles),
        out_shape=[
            jax.ShapeDtypeStruct((cycles, BLK, P_SIZE), F32),
            jax.ShapeDtypeStruct((cycles, BLK), F32),
        ],
        in_specs=[pl.BlockSpec(memory_space=pltpu.VMEM)],
        out_specs=[pl.BlockSpec(memory_space=pltpu.VMEM)] * 2,
        compiler_params=pltpu.CompilerParams(vmem_limit_bytes=24 * 2**20),
        cost_estimate=pl.CostEstimate(
            flops=20 * 2**20, bytes_accessed=3 * 2**20, transcendentals=2 * 2**20
        ),
    )(pieces.reshape(groups, cycles, *pieces.shape[1:]))


def spread_panel(x, info, core, start):
    ring = lax.axis_size("items")
    chips = ring // CORES
    half = x.shape[0] // CORES
    across = [(i, i ^ 1) for i in range(ring)]

    def step(block, distance):
        pairs = [
            (y * CORES + c, (y + distance) % chips * CORES + c)
            for y in range(chips)
            for c in range(CORES)
        ]
        return lax.ppermute(block, "items", pairs)

    own = lax.dynamic_slice(x, (core * half, start), (half, P_SIZE))
    other = lax.dynamic_slice(x, ((1 - core) * half, start), (half, P_SIZE))
    mine = select(choose_kernel, info, own, lax.ppermute(other, "items", across))
    right, left = step(mine, 1), step(mine, -1)
    first, second = turn(right, left, touch(x, mine))
    far_a, far_b = step(first, 1), step(second, -1)
    mine = select(join_kernel, info, mine, right, left, far_a, far_b)
    return mine, lax.ppermute(mine, "items", across)


def per_device(interactions, user_weights, panel_index):
    groups, ring = lax.axis_size("users"), lax.axis_size("items")
    me, chips = lax.axis_index("items"), ring // CORES
    per_shard = interactions.shape[1] // P_SIZE
    owner, place = panel_index[0] // per_shard, panel_index[0] % per_shard
    core = me % CORES
    away = (me // CORES - owner // CORES) % chips
    same = (core == owner % CORES).astype(jnp.int32)
    info = jnp.stack([core, away, same]).astype(jnp.int32)
    mine, other = spread_panel(interactions, info, core, place * P_SIZE)
    pieces = moments(info, interactions, mine, other, user_weights, groups * ring)
    moved = lax.all_to_all(pieces, ("users", "items"), 0, 0, tiled=True)
    return tuple(merge(moved, groups, ring))


def solution(mesh):
    return jax.shard_map(
        per_device,
        mesh=mesh,
        in_specs=(P("users", "items"), P("users"), P()),
        out_specs=(P(None, ("users", "items"), None), P(None, ("users", "items"))),
        check_vma=False,
    )
```

```python
import functools

import jax
import jax.numpy as jnp
from jax import lax
from jax.experimental import pallas as pl
from jax.experimental.pallas import tpu as pltpu
from jax.sharding import Mesh
from jax.sharding import PartitionSpec as P

P_SIZE = 256
BLK = 32
LANES = 128
CORES = 2
USERS, ITEMS = ("z", "x"), ("y", "c")
ORDER = ("c", "y", "x", "z")
CORE, AWAY, SAME = range(3)
EXTRA = 8
F32 = jnp.float32
BF16 = jnp.bfloat16


def slot(owner):
    place = dict(zip(USERS + ITEMS, (owner // 32, owner // 8 % 4, owner // 2 % 4, owner % 2)))
    index = 0
    for axis in ORDER:
        index = index * (CORES if axis == "c" else 4) + place[axis]
    return index


def split3(value):
    parts = []
    for _ in range(3):
        part = value.astype(BF16).astype(F32)
        parts.append(part)
        value = value - part
    return parts


def touch_kernel(x_ref, after_ref, out_ref):
    out_ref[...] = jnp.zeros_like(out_ref)


def touch(x, after):
    return pl.pallas_call(
        touch_kernel,
        in_specs=[pl.BlockSpec(memory_space=pltpu.VMEM), pl.BlockSpec(memory_space=pl.ANY)],
        out_specs=pl.BlockSpec(memory_space=pltpu.VMEM),
        out_shape=jax.ShapeDtypeStruct((8, LANES), F32),
        compiler_params=pltpu.CompilerParams(vmem_limit_bytes=2 * 2**20),
        cost_estimate=pl.CostEstimate(
            flops=0, bytes_accessed=x.size * x.dtype.itemsize, transcendentals=0
        ),
    )(x, after)


def turn_kernel(right_ref, left_ref, after_ref, first_ref, second_ref):
    part = first_ref.shape[0]
    first_ref[...] = right_ref[0:part, :]
    second_ref[...] = left_ref[part:, :]


def turn(right, left, after):
    rows, columns = right.shape
    shape = jax.ShapeDtypeStruct((rows // 2, columns), right.dtype)
    return pl.pallas_call(
        turn_kernel,
        in_specs=[pl.BlockSpec(memory_space=pltpu.VMEM)] * 2 + [pl.BlockSpec(memory_space=pl.ANY)],
        out_specs=[pl.BlockSpec(memory_space=pltpu.VMEM)] * 2,
        out_shape=[shape, shape],
        compiler_params=pltpu.CompilerParams(vmem_limit_bytes=4 * 2**20),
        cost_estimate=pl.CostEstimate(flops=0, bytes_accessed=2**20, transcendentals=0),
    )(right, left, after)


def choose_kernel(info_ref, own_ref, got_ref, out_ref):
    @pl.when(info_ref[SAME] == 1)
    def _():
        out_ref[...] = own_ref[...]

    @pl.when(info_ref[SAME] != 1)
    def _():
        out_ref[...] = got_ref[...]


def join_kernel(info_ref, mine_ref, right_ref, left_ref, far_a_ref, far_b_ref, out_ref):
    part = far_a_ref.shape[0]
    for k, ref in ((0, mine_ref), (1, right_ref), (3, left_ref)):

        @pl.when(info_ref[AWAY] == k)
        def _():
            out_ref[...] = ref[...]

    @pl.when(info_ref[AWAY] == 2)
    def _():
        out_ref[0:part, :] = far_a_ref[...]
        out_ref[part:, :] = far_b_ref[...]


def select(kernel, info, *blocks):
    return pl.pallas_call(
        kernel,
        in_specs=[pl.BlockSpec(memory_space=pltpu.SMEM)]
        + [pl.BlockSpec(memory_space=pltpu.VMEM)] * len(blocks),
        out_specs=pl.BlockSpec(memory_space=pltpu.VMEM),
        out_shape=jax.ShapeDtypeStruct(blocks[0].shape, blocks[0].dtype),
        compiler_params=pltpu.CompilerParams(vmem_limit_bytes=2 * 2**20),
        cost_estimate=pl.CostEstimate(flops=0, bytes_accessed=2**20, transcendentals=0),
    )(info, *blocks)


def left_side(core, w_ref, block_ref, lhs):
    half = block_ref.shape[0]
    lanes16 = w_ref[...].astype(F32)
    per = half // LANES
    rows = jnp.where(core == 0, lanes16[0:per], lanes16[per:])
    wrow = jnp.concatenate([rows[k : k + 1, :] for k in range(per)], axis=1)
    product = block_ref[...].T.astype(F32) * wrow
    lhs[0:P_SIZE, :] = product.astype(BF16)
    lhs[P_SIZE:, :] = jnp.broadcast_to(wrow, (16, half)).astype(BF16)
    total = product[:, 0:LANES]
    for g in range(LANES, half, LANES):
        total += product[:, g : g + LANES]
    return total


def own_kernel(tile, info_ref, w_ref, block_ref, x_ref, acc_ref, total_ref, lhs):
    half, core = block_ref.shape[0], info_ref[CORE]
    total_ref[...] = left_side(core, w_ref, block_ref, lhs)
    users = pl.ds(pl.multiple_of(core * half, half), half)
    for t in range(x_ref.shape[1] // tile):
        cut = slice(t * tile, (t + 1) * tile)
        acc_ref[:, cut] = jnp.dot(lhs[...], x_ref[users, cut], preferred_element_type=F32)


def own_half(info, x, block, weights):
    users, items = x.shape
    return pl.pallas_call(
        functools.partial(own_kernel, 512),
        in_specs=[pl.BlockSpec(memory_space=pltpu.SMEM)]
        + [pl.BlockSpec(memory_space=pltpu.VMEM)] * 3,
        out_specs=[pl.BlockSpec(memory_space=pltpu.VMEM)] * 2,
        out_shape=[
            jax.ShapeDtypeStruct((P_SIZE + 16, items), F32),
            jax.ShapeDtypeStruct((P_SIZE, LANES), F32),
        ],
        scratch_shapes=[pltpu.VMEM((P_SIZE + 16, users // CORES), BF16)],
        compiler_params=pltpu.CompilerParams(vmem_limit_bytes=12 * 2**20),
        cost_estimate=pl.CostEstimate(
            flops=users * items * P_SIZE, bytes_accessed=4 * 2**20, transcendentals=0
        ),
    )(info, weights.reshape(-1, LANES), block, x)


def moment_kernel(
    tile, info_ref, w_ref, block_ref, x_ref, acc_ref, total_ref, out_ref, lhs
):
    items = x_ref.shape[1]
    half, core = block_ref.shape[0], 1 - info_ref[CORE]
    total = total_ref[...] + left_side(core, w_ref, block_ref, lhs)
    users = pl.ds(pl.multiple_of(core * half, half), half)
    weights = w_ref[...].astype(F32)
    count = jnp.sum(jnp.sum(weights, axis=0, keepdims=True), axis=1, keepdims=True)
    inverse = 1.0 / count
    pcol = jnp.sum(total, axis=1, keepdims=True) * inverse
    prow = jnp.broadcast_to(pcol, (P_SIZE, LANES)).T[0:1, :]
    hi, mid, lo = split3(prow)
    chi, cmid, clo = split3(jnp.broadcast_to(count, (1, LANES)))
    rows = [v[:, h : h + LANES] for v in (hi, mid, lo) for h in (0, LANES)]
    lane1 = lax.broadcasted_iota(jnp.int32, (1, LANES), 1)
    last = jnp.where(lane1 < 32, chi, jnp.where(lane1 < 64, cmid, clo))
    fixed = jnp.concatenate(rows + [last, last], axis=0)
    lane = lax.broadcasted_iota(jnp.int32, (1, tile), 1) % LANES
    lane8 = lax.broadcasted_iota(jnp.int32, (EXTRA, LANES), 1)
    row8 = lax.broadcasted_iota(jnp.int32, (EXTRA, LANES), 0)
    per = LANES // BLK
    pieces = tile // BLK

    for t in range(items // tile):
        cut = slice(t * tile, (t + 1) * tile)
        acc = acc_ref[:, cut] + jnp.dot(
            lhs[...], x_ref[users, cut], preferred_element_type=F32
        )
        mrow = acc[P_SIZE : P_SIZE + 1, :] * inverse
        moment = acc[0:P_SIZE, :] * inverse - pcol * mrow
        top = jnp.max(jnp.max(jnp.abs(moment), axis=0, keepdims=True), axis=1, keepdims=True)
        scale = (32768.0 / jnp.maximum(top, 1e-30)).astype(BF16).astype(F32)
        v = moment * scale
        v2 = v * v
        coded = (v * jnp.abs(v) * v2 * (v2 * v2)).astype(BF16).T.reshape(pieces, BLK, P_SIZE)
        for k in range(pieces):
            place = slot(t * pieces + k)
            out_ref[place, 0:BLK, :] = coded[k, :, 0:LANES]
            out_ref[place, BLK : 2 * BLK, :] = coded[k, :, LANES:]
        hi, mid, lo = split3(mrow)
        base = jnp.where((row8 == 7) & (lane8 >= 96), scale, fixed)
        for q in range(per):
            mix = jnp.where(
                lane < 32,
                pltpu.roll(hi, (tile - 32 * q) % tile, 1),
                jnp.where(
                    lane < 64,
                    pltpu.roll(mid, (tile + 32 - 32 * q) % tile, 1),
                    pltpu.roll(lo, (tile + 64 - 32 * q) % tile, 1),
                ),
            )
            for g in range(tile // LANES):
                row = jnp.broadcast_to(mix[:, g * LANES : (g + 1) * LANES], (EXTRA, LANES))
                stats = jnp.where(row8 == 6, row, base).astype(BF16)
                out_ref[slot(t * pieces + g * per + q), 2 * BLK :, :] = stats


def moments(info, x, mine, other, weights, pieces):
    acc, total = own_half(info, x, mine, weights)
    users, items = x.shape
    tile = 512
    return pl.pallas_call(
        functools.partial(moment_kernel, tile),
        in_specs=[pl.BlockSpec(memory_space=pltpu.SMEM)]
        + [pl.BlockSpec(memory_space=pltpu.VMEM)] * 5,
        out_specs=pl.BlockSpec(memory_space=pltpu.VMEM),
        out_shape=jax.ShapeDtypeStruct((pieces, 2 * BLK + EXTRA, LANES), BF16),
        scratch_shapes=[pltpu.VMEM((P_SIZE + 16, users // CORES), BF16)],
        compiler_params=pltpu.CompilerParams(vmem_limit_bytes=16 * 2**20),
        cost_estimate=pl.CostEstimate(
            flops=users * items * P_SIZE, bytes_accessed=4 * 2**20, transcendentals=0
        ),
    )(info, weights.reshape(-1, LANES), other, x, acc, total)


def merge_kernel(groups, cycles, in_ref, cov_ref, mean_ref):
    stats0 = in_ref[0, :, 2 * BLK :, :].astype(F32)
    part = lambda row: jnp.concatenate([stats0[:, row, :], stats0[:, row + 1, :]], axis=1)
    panel = part(0) + part(2) + part(4)
    last = stats0[:, 7, :]
    count = last[:, 0:1] + last[:, 32:33] + last[:, 64:65]
    share = count / jnp.sum(count, axis=0, keepdims=True)
    panel_dev = panel - jnp.sum(share * panel, axis=0, keepdims=True)
    for i in range(cycles):
        at = i % CORES * (cycles // CORES) + i // CORES
        stats = in_ref[at, :, 2 * BLK :, :].astype(F32)
        row = stats[:, 6, :]
        mean = row[:, 0:32] + row[:, 32:64] + row[:, 64:96]
        mean_all = jnp.sum(share * mean, axis=0, keepdims=True)
        mean_ref[i : i + 1, :] = mean_all
        left = jnp.broadcast_to(share, (groups, 32)) * (mean - mean_all)
        between = lax.dot_general(
            left,
            panel_dev,
            (((0,), (0,)), ((), ())),
            precision=lax.Precision.HIGHEST,
            preferred_element_type=F32,
        )
        back = share / stats[:, 7, 96:97]
        within = jnp.zeros((2 * BLK, LANES), F32)
        for u in range(groups):
            y = in_ref[at, u, 0 : 2 * BLK, :].astype(F32)
            shrink = jnp.exp2(-0.875 * jnp.log2(jnp.maximum(jnp.abs(y), 1e-37)))
            within = within + (y * back[u : u + 1, :]) * shrink
        first = within[0:BLK] + between[:, 0:LANES]
        second = within[BLK:] + between[:, LANES:]
        cov_ref[i, :, 0:LANES] = first
        cov_ref[i, :, LANES:] = second


def merge(pieces, groups, cycles):
    return pl.pallas_call(
        functools.partial(merge_kernel, groups, cycles),
        out_shape=[
            jax.ShapeDtypeStruct((cycles, BLK, P_SIZE), F32),
            jax.ShapeDtypeStruct((cycles, BLK), F32),
        ],
        in_specs=[pl.BlockSpec(memory_space=pltpu.VMEM)],
        out_specs=[pl.BlockSpec(memory_space=pltpu.VMEM)] * 2,
        compiler_params=pltpu.CompilerParams(vmem_limit_bytes=24 * 2**20),
        cost_estimate=pl.CostEstimate(
            flops=20 * 2**20, bytes_accessed=3 * 2**20, transcendentals=2 * 2**20
        ),
    )(pieces.reshape(cycles, groups, *pieces.shape[1:]))


def spread_panel(x, info, core, start):
    ring = lax.axis_size(ITEMS)
    chips = ring // CORES
    half = x.shape[0] // CORES
    across = [(i, i ^ 1) for i in range(ring)]

    def step(block, distance):
        pairs = [
            (y * CORES + c, (y + distance) % chips * CORES + c)
            for y in range(chips)
            for c in range(CORES)
        ]
        return lax.ppermute(block, ITEMS, pairs)

    own = lax.dynamic_slice(x, (core * half, start), (half, P_SIZE))
    other = lax.dynamic_slice(x, ((1 - core) * half, start), (half, P_SIZE))
    mine = select(choose_kernel, info, own, lax.ppermute(other, ITEMS, across))
    right, left = step(mine, 1), step(mine, -1)
    first, second = turn(right, left, touch(x, mine))
    far_a, far_b = step(first, 1), step(second, -1)
    mine = select(join_kernel, info, mine, right, left, far_a, far_b)
    return mine, lax.ppermute(mine, ITEMS, across)


def per_device(interactions, user_weights, panel_index):
    groups, ring = lax.axis_size(USERS), lax.axis_size(ITEMS)
    me, chips = lax.axis_index(ITEMS), ring // CORES
    per_shard = interactions.shape[1] // P_SIZE
    owner, place = panel_index[0] // per_shard, panel_index[0] % per_shard
    core = me % CORES
    away = (me // CORES - owner // CORES) % chips
    same = (core == owner % CORES).astype(jnp.int32)
    info = jnp.stack([core, away, same]).astype(jnp.int32)
    mine, other = spread_panel(interactions, info, core, place * P_SIZE)
    pieces = moments(info, interactions, mine, other, user_weights, groups * ring)
    moved = lax.all_to_all(pieces, ORDER, 0, 0, tiled=True)
    return tuple(merge(moved, groups, ring))


def solution(mesh):
    split = Mesh(mesh.devices.reshape(4, 4, 4, CORES), USERS + ITEMS)
    return jax.shard_map(
        per_device,
        mesh=split,
        in_specs=(P(USERS, ITEMS), P(USERS), P()),
        out_specs=(P(None, USERS + ITEMS, None), P(None, USERS + ITEMS)),
        check_vma=False,
    )
```

```python
import functools

import jax
import jax.numpy as jnp
from jax import lax
from jax.experimental import pallas as pl
from jax.experimental.pallas import tpu as pltpu
from jax.sharding import Mesh
from jax.sharding import PartitionSpec as P

P_SIZE = 256
BLK = 32
LANES = 128
CORES = 2
USERS, ITEMS = ("z", "x"), ("y", "c")
ORDER = ("c", "y", "x", "z")
CORE, AWAY = range(2)
EXTRA = 8
F32 = jnp.float32
BF16 = jnp.bfloat16


def slot(owner):
    place = dict(zip(USERS + ITEMS, (owner // 32, owner // 8 % 4, owner // 2 % 4, owner % 2)))
    index = 0
    for axis in ORDER:
        index = index * (CORES if axis == "c" else 4) + place[axis]
    return index


def split3(value):
    parts = []
    for _ in range(3):
        part = value.astype(BF16).astype(F32)
        parts.append(part)
        value = value - part
    return parts


def touch_kernel(x_ref, after_ref, info_ref, out_ref):
    out_ref[...] = jnp.zeros_like(out_ref)


def touch(x, *after):
    return pl.pallas_call(
        touch_kernel,
        in_specs=[pl.BlockSpec(memory_space=pltpu.VMEM)] + [pl.BlockSpec(memory_space=pl.ANY)] * 2,
        out_specs=pl.BlockSpec(memory_space=pltpu.VMEM),
        out_shape=jax.ShapeDtypeStruct((8, LANES), F32),
        compiler_params=pltpu.CompilerParams(vmem_limit_bytes=2 * 2**20),
        cost_estimate=pl.CostEstimate(
            flops=0, bytes_accessed=x.size * x.dtype.itemsize, transcendentals=0
        ),
    )(x, *after)


def turn_kernel(right_ref, left_ref, after_ref, first_ref, second_ref):
    part = first_ref.shape[0]
    first_ref[...] = right_ref[0:part, :]
    second_ref[...] = left_ref[part:, :]


def turn(right, left, after):
    rows, columns = right.shape
    shape = jax.ShapeDtypeStruct((rows // 2, columns), right.dtype)
    return pl.pallas_call(
        turn_kernel,
        in_specs=[pl.BlockSpec(memory_space=pltpu.VMEM)] * 2 + [pl.BlockSpec(memory_space=pl.ANY)],
        out_specs=[pl.BlockSpec(memory_space=pltpu.VMEM)] * 2,
        out_shape=[shape, shape],
        compiler_params=pltpu.CompilerParams(vmem_limit_bytes=4 * 2**20),
        cost_estimate=pl.CostEstimate(flops=0, bytes_accessed=2**20, transcendentals=0),
    )(right, left, after)


def join_kernel(info_ref, mine_ref, right_ref, left_ref, far_a_ref, far_b_ref, out_ref):
    part = far_a_ref.shape[0]
    for k, ref in ((0, mine_ref), (1, right_ref), (3, left_ref)):

        @pl.when(info_ref[AWAY] == k)
        def _():
            out_ref[...] = ref[...]

    @pl.when(info_ref[AWAY] == 2)
    def _():
        out_ref[0:part, :] = far_a_ref[...]
        out_ref[part:, :] = far_b_ref[...]


def join(info, *blocks):
    return pl.pallas_call(
        join_kernel,
        in_specs=[pl.BlockSpec(memory_space=pltpu.SMEM)]
        + [pl.BlockSpec(memory_space=pltpu.VMEM)] * len(blocks),
        out_specs=pl.BlockSpec(memory_space=pltpu.VMEM),
        out_shape=jax.ShapeDtypeStruct(blocks[0].shape, blocks[0].dtype),
        compiler_params=pltpu.CompilerParams(vmem_limit_bytes=2 * 2**20),
        cost_estimate=pl.CostEstimate(flops=0, bytes_accessed=2**20, transcendentals=0),
    )(info, *blocks)


def left_side(core, w_ref, block_ref, lhs):
    half = block_ref.shape[0]
    lanes16 = w_ref[...].astype(F32)
    per = half // LANES
    rows = jnp.where(core == 0, lanes16[0:per], lanes16[per:])
    wrow = jnp.concatenate([rows[k : k + 1, :] for k in range(per)], axis=1)
    product = block_ref[...].T.astype(F32) * wrow
    lhs[0:P_SIZE, :] = product.astype(BF16)
    lhs[P_SIZE:, :] = jnp.broadcast_to(wrow, (16, half)).astype(BF16)
    total = product[:, 0:LANES]
    for g in range(LANES, half, LANES):
        total += product[:, g : g + LANES]
    return total


def own_kernel(tile, info_ref, w_ref, block_ref, x_ref, acc_ref, total_ref, lhs):
    half, core = block_ref.shape[0], info_ref[CORE]
    total_ref[...] = left_side(core, w_ref, block_ref, lhs)
    users = pl.ds(pl.multiple_of(core * half, half), half)
    for t in range(x_ref.shape[1] // tile):
        cut = slice(t * tile, (t + 1) * tile)
        acc_ref[:, cut] = jnp.dot(lhs[...], x_ref[users, cut], preferred_element_type=F32)


def own_half(info, x, block, weights):
    users, items = x.shape
    return pl.pallas_call(
        functools.partial(own_kernel, 512),
        in_specs=[pl.BlockSpec(memory_space=pltpu.SMEM)]
        + [pl.BlockSpec(memory_space=pltpu.VMEM)] * 3,
        out_specs=[pl.BlockSpec(memory_space=pltpu.VMEM)] * 2,
        out_shape=[
            jax.ShapeDtypeStruct((P_SIZE + 16, items), F32),
            jax.ShapeDtypeStruct((P_SIZE, LANES), F32),
        ],
        scratch_shapes=[pltpu.VMEM((P_SIZE + 16, users // CORES), BF16)],
        compiler_params=pltpu.CompilerParams(vmem_limit_bytes=12 * 2**20),
        cost_estimate=pl.CostEstimate(
            flops=users * items * P_SIZE, bytes_accessed=4 * 2**20, transcendentals=0
        ),
    )(info, weights.reshape(-1, LANES), block, x)


def moment_kernel(
    tile, info_ref, w_ref, block_ref, x_ref, acc_ref, total_ref, out_ref, lhs
):
    items = x_ref.shape[1]
    half, core = block_ref.shape[0], 1 - info_ref[CORE]
    total = total_ref[...] + left_side(core, w_ref, block_ref, lhs)
    users = pl.ds(pl.multiple_of(core * half, half), half)
    weights = w_ref[...].astype(F32)
    count = jnp.sum(jnp.sum(weights, axis=0, keepdims=True), axis=1, keepdims=True)
    inverse = 1.0 / count
    pcol = jnp.sum(total, axis=1, keepdims=True) * inverse
    prow = jnp.broadcast_to(pcol, (P_SIZE, LANES)).T[0:1, :]
    hi, mid, lo = split3(prow)
    chi, cmid, clo = split3(jnp.broadcast_to(count, (1, LANES)))
    rows = [v[:, h : h + LANES] for v in (hi, mid, lo) for h in (0, LANES)]
    lane1 = lax.broadcasted_iota(jnp.int32, (1, LANES), 1)
    last = jnp.where(lane1 < 32, chi, jnp.where(lane1 < 64, cmid, clo))
    fixed = jnp.concatenate(rows + [last, last], axis=0)
    lane = lax.broadcasted_iota(jnp.int32, (1, tile), 1) % LANES
    lane8 = lax.broadcasted_iota(jnp.int32, (EXTRA, LANES), 1)
    row8 = lax.broadcasted_iota(jnp.int32, (EXTRA, LANES), 0)
    per = LANES // BLK
    pieces = tile // BLK

    def whole(t):
        cut = slice(t * tile, (t + 1) * tile)
        return acc_ref[:, cut] + jnp.dot(
            lhs[...], x_ref[users, cut], preferred_element_type=F32
        )

    later = whole(0)
    for t in range(items // tile):
        acc = later
        if t + 1 < items // tile:
            later = whole(t + 1)
        mrow = acc[P_SIZE : P_SIZE + 1, :] * inverse
        moment = acc[0:P_SIZE, :] * inverse - pcol * mrow
        top = jnp.max(jnp.max(jnp.abs(moment), axis=0, keepdims=True), axis=1, keepdims=True)
        scale = (32768.0 / jnp.maximum(top, 1e-30)).astype(BF16).astype(F32)
        v = moment * scale
        v2 = v * v
        coded = (v * jnp.abs(v) * v2 * (v2 * v2)).astype(BF16).T.reshape(pieces, BLK, P_SIZE)
        for k in range(pieces):
            place = slot(t * pieces + k)
            out_ref[place, 0:BLK, :] = coded[k, :, 0:LANES]
            out_ref[place, BLK : 2 * BLK, :] = coded[k, :, LANES:]
        hi, mid, lo = split3(mrow)
        base = jnp.where((row8 == 7) & (lane8 >= 96), scale, fixed)
        for q in range(per):
            mix = jnp.where(
                lane < 32,
                pltpu.roll(hi, (tile - 32 * q) % tile, 1),
                jnp.where(
                    lane < 64,
                    pltpu.roll(mid, (tile + 32 - 32 * q) % tile, 1),
                    pltpu.roll(lo, (tile + 64 - 32 * q) % tile, 1),
                ),
            )
            for g in range(tile // LANES):
                row = jnp.broadcast_to(mix[:, g * LANES : (g + 1) * LANES], (EXTRA, LANES))
                stats = jnp.where(row8 == 6, row, base).astype(BF16)
                out_ref[slot(t * pieces + g * per + q), 2 * BLK :, :] = stats


def moments(info, x, mine, other, weights, pieces):
    acc, total = own_half(info, x, mine, weights)
    users, items = x.shape
    tile = 512
    return pl.pallas_call(
        functools.partial(moment_kernel, tile),
        in_specs=[pl.BlockSpec(memory_space=pltpu.SMEM)]
        + [pl.BlockSpec(memory_space=pltpu.VMEM)] * 5,
        out_specs=pl.BlockSpec(memory_space=pltpu.VMEM),
        out_shape=jax.ShapeDtypeStruct((pieces, 2 * BLK + EXTRA, LANES), BF16),
        scratch_shapes=[pltpu.VMEM((P_SIZE + 16, users // CORES), BF16)],
        compiler_params=pltpu.CompilerParams(vmem_limit_bytes=16 * 2**20),
        cost_estimate=pl.CostEstimate(
            flops=users * items * P_SIZE, bytes_accessed=4 * 2**20, transcendentals=0
        ),
    )(info, weights.reshape(-1, LANES), other, x, acc, total)


def merge_kernel(groups, cycles, in_ref, cov_ref, mean_ref):
    stats0 = in_ref[0, :, 2 * BLK :, :].astype(F32)
    part = lambda row: jnp.concatenate([stats0[:, row, :], stats0[:, row + 1, :]], axis=1)
    panel = part(0) + part(2) + part(4)
    last = stats0[:, 7, :]
    count = last[:, 0:1] + last[:, 32:33] + last[:, 64:65]
    share = count / jnp.sum(count, axis=0, keepdims=True)
    panel_dev = panel - jnp.sum(share * panel, axis=0, keepdims=True)
    for i in range(cycles):
        at = i % CORES * (cycles // CORES) + i // CORES
        stats = in_ref[at, :, 2 * BLK :, :].astype(F32)
        row = stats[:, 6, :]
        mean = row[:, 0:32] + row[:, 32:64] + row[:, 64:96]
        mean_all = jnp.sum(share * mean, axis=0, keepdims=True)
        mean_ref[i : i + 1, :] = mean_all
        left = jnp.broadcast_to(share, (groups, 32)) * (mean - mean_all)
        between = lax.dot_general(
            left,
            panel_dev,
            (((0,), (0,)), ((), ())),
            precision=lax.Precision.HIGHEST,
            preferred_element_type=F32,
        )
        back = share / stats[:, 7, 96:97]
        within = jnp.zeros((2 * BLK, LANES), F32)
        for u in range(groups):
            y = in_ref[at, u, 0 : 2 * BLK, :].astype(F32)
            shrink = jnp.exp2(-0.875 * jnp.log2(jnp.maximum(jnp.abs(y), 1e-37)))
            within = within + (y * back[u : u + 1, :]) * shrink
        first = within[0:BLK] + between[:, 0:LANES]
        second = within[BLK:] + between[:, LANES:]
        cov_ref[i, :, 0:LANES] = first
        cov_ref[i, :, LANES:] = second


def merge(pieces, groups, cycles):
    return pl.pallas_call(
        functools.partial(merge_kernel, groups, cycles),
        out_shape=[
            jax.ShapeDtypeStruct((cycles, BLK, P_SIZE), F32),
            jax.ShapeDtypeStruct((cycles, BLK), F32),
        ],
        in_specs=[pl.BlockSpec(memory_space=pltpu.VMEM)],
        out_specs=[pl.BlockSpec(memory_space=pltpu.VMEM)] * 2,
        compiler_params=pltpu.CompilerParams(vmem_limit_bytes=24 * 2**20),
        cost_estimate=pl.CostEstimate(
            flops=20 * 2**20, bytes_accessed=3 * 2**20, transcendentals=2 * 2**20
        ),
    )(pieces.reshape(cycles, groups, *pieces.shape[1:]))


def spread_panel(x, info, core, same, start):
    ring = lax.axis_size(ITEMS)
    chips = ring // CORES
    half = x.shape[0] // CORES
    across = [(i, i ^ 1) for i in range(ring)]

    def step(block, distance):
        pairs = [
            (y * CORES + c, (y + distance) % chips * CORES + c)
            for y in range(chips)
            for c in range(CORES)
        ]
        return lax.ppermute(block, ITEMS, pairs)

    own = lax.dynamic_slice(x, (core * half, start), (half, P_SIZE))
    other = lax.dynamic_slice(x, ((1 - core) * half, start), (half, P_SIZE))
    own, other = lax.optimization_barrier((own, other))
    mine = jnp.where(same, own, lax.ppermute(other, ITEMS, across))
    right, left = step(mine, 1), step(mine, -1)
    first, second = turn(right, left, touch(x, mine, info))
    far_a, far_b = step(first, 1), step(second, -1)
    mine = join(info, mine, right, left, far_a, far_b)
    return mine, lax.ppermute(mine, ITEMS, across)


def per_device(interactions, user_weights, panel_index):
    groups, ring = lax.axis_size(USERS), lax.axis_size(ITEMS)
    me, chips = lax.axis_index(ITEMS), ring // CORES
    per_shard = interactions.shape[1] // P_SIZE
    owner, place = panel_index[0] // per_shard, panel_index[0] % per_shard
    core = me % CORES
    away = (me // CORES - owner // CORES) % chips
    same = core == owner % CORES
    info = jnp.stack([core, away]).astype(jnp.int32)
    mine, other = spread_panel(interactions, info, core, same, place * P_SIZE)
    pieces = moments(info, interactions, mine, other, user_weights, groups * ring)
    moved = lax.all_to_all(pieces, ORDER, 0, 0, tiled=True)
    return tuple(merge(moved, groups, ring))


def solution(mesh):
    split = Mesh(mesh.devices.reshape(4, 4, 4, CORES), USERS + ITEMS)
    return jax.shard_map(
        per_device,
        mesh=split,
        in_specs=(P(USERS, ITEMS), P(USERS), P()),
        out_specs=(P(None, USERS + ITEMS, None), P(None, USERS + ITEMS)),
        check_vma=False,
    )
```

```python
import functools

import jax
import jax.numpy as jnp
from jax import lax
from jax.experimental import pallas as pl
from jax.experimental.pallas import tpu as pltpu
from jax.sharding import Mesh
from jax.sharding import PartitionSpec as P

P_SIZE = 256
BLK = 32
LANES = 128
CORES = 2
USERS, ITEMS = ("z", "x"), ("y", "c")
ORDER = ("c", "y", "x", "z")
CORE, AWAY = range(2)
EXTRA = 8
F32 = jnp.float32
BF16 = jnp.bfloat16


def slot(owner):
    place = dict(zip(USERS + ITEMS, (owner // 32, owner // 8 % 4, owner // 2 % 4, owner % 2)))
    index = 0
    for axis in ORDER:
        index = index * (CORES if axis == "c" else 4) + place[axis]
    return index


def split3(value):
    parts = []
    for _ in range(3):
        part = value.astype(BF16).astype(F32)
        parts.append(part)
        value = value - part
    return parts


def touch_kernel(x_ref, after_ref, info_ref, out_ref):
    out_ref[...] = jnp.zeros_like(out_ref)


def touch(x, *after):
    return pl.pallas_call(
        touch_kernel,
        in_specs=[pl.BlockSpec(memory_space=pltpu.VMEM)] + [pl.BlockSpec(memory_space=pl.ANY)] * 2,
        out_specs=pl.BlockSpec(memory_space=pltpu.VMEM),
        out_shape=jax.ShapeDtypeStruct((8, LANES), F32),
        compiler_params=pltpu.CompilerParams(vmem_limit_bytes=2 * 2**20),
        cost_estimate=pl.CostEstimate(
            flops=0, bytes_accessed=x.size * x.dtype.itemsize, transcendentals=0
        ),
    )(x, *after)


def turn_kernel(right_ref, left_ref, after_ref, first_ref, second_ref):
    part = first_ref.shape[0]
    first_ref[...] = right_ref[0:part, :]
    second_ref[...] = left_ref[part:, :]


def turn(right, left, after):
    rows, columns = right.shape
    shape = jax.ShapeDtypeStruct((rows // 2, columns), right.dtype)
    return pl.pallas_call(
        turn_kernel,
        in_specs=[pl.BlockSpec(memory_space=pltpu.VMEM)] * 2 + [pl.BlockSpec(memory_space=pl.ANY)],
        out_specs=[pl.BlockSpec(memory_space=pltpu.VMEM)] * 2,
        out_shape=[shape, shape],
        compiler_params=pltpu.CompilerParams(vmem_limit_bytes=4 * 2**20),
        cost_estimate=pl.CostEstimate(flops=0, bytes_accessed=2**20, transcendentals=0),
    )(right, left, after)


def join_kernel(info_ref, mine_ref, right_ref, left_ref, far_a_ref, far_b_ref, out_ref):
    part = far_a_ref.shape[0]
    for k, ref in ((0, mine_ref), (1, right_ref), (3, left_ref)):

        @pl.when(info_ref[AWAY] == k)
        def _():
            out_ref[...] = ref[...]

    @pl.when(info_ref[AWAY] == 2)
    def _():
        out_ref[0:part, :] = far_a_ref[...]
        out_ref[part:, :] = far_b_ref[...]


def join(info, *blocks):
    return pl.pallas_call(
        join_kernel,
        in_specs=[pl.BlockSpec(memory_space=pltpu.SMEM)]
        + [pl.BlockSpec(memory_space=pltpu.VMEM)] * len(blocks),
        out_specs=pl.BlockSpec(memory_space=pltpu.VMEM),
        out_shape=jax.ShapeDtypeStruct(blocks[0].shape, blocks[0].dtype),
        compiler_params=pltpu.CompilerParams(vmem_limit_bytes=2 * 2**20),
        cost_estimate=pl.CostEstimate(flops=0, bytes_accessed=2**20, transcendentals=0),
    )(info, *blocks)


def left_side(core, w_ref, block_ref, lhs):
    half = block_ref.shape[0]
    lanes16 = w_ref[...].astype(F32)
    per = half // LANES
    rows = jnp.where(core == 0, lanes16[0:per], lanes16[per:])
    wrow = jnp.concatenate([rows[k : k + 1, :] for k in range(per)], axis=1)
    product = block_ref[...].T.astype(F32) * wrow
    lhs[0:P_SIZE, :] = product.astype(BF16)
    lhs[P_SIZE:, :] = jnp.broadcast_to(wrow, (16, half)).astype(BF16)
    total = product[:, 0:LANES]
    for g in range(LANES, half, LANES):
        total += product[:, g : g + LANES]
    return total


def own_kernel(tile, info_ref, w_ref, block_ref, x_ref, acc_ref, total_ref, lhs):
    half, core = block_ref.shape[0], info_ref[CORE]
    total_ref[...] = left_side(core, w_ref, block_ref, lhs)
    users = pl.ds(pl.multiple_of(core * half, half), half)
    for t in range(x_ref.shape[1] // tile):
        cut = slice(t * tile, (t + 1) * tile)
        acc_ref[:, cut] = jnp.dot(lhs[...], x_ref[users, cut], preferred_element_type=F32)


def own_half(info, x, block, weights):
    users, items = x.shape
    return pl.pallas_call(
        functools.partial(own_kernel, 512),
        in_specs=[pl.BlockSpec(memory_space=pltpu.SMEM)]
        + [pl.BlockSpec(memory_space=pltpu.VMEM)] * 3,
        out_specs=[pl.BlockSpec(memory_space=pltpu.VMEM)] * 2,
        out_shape=[
            jax.ShapeDtypeStruct((P_SIZE + 16, items), F32),
            jax.ShapeDtypeStruct((P_SIZE, LANES), F32),
        ],
        scratch_shapes=[pltpu.VMEM((P_SIZE + 16, users // CORES), BF16)],
        compiler_params=pltpu.CompilerParams(vmem_limit_bytes=12 * 2**20),
        cost_estimate=pl.CostEstimate(
            flops=users * items * P_SIZE, bytes_accessed=4 * 2**20, transcendentals=0
        ),
    )(info, weights.reshape(-1, LANES), block, x)


def moment_kernel(
    tile, info_ref, w_ref, block_ref, x_ref, acc_ref, total_ref, out_ref, lhs
):
    items = x_ref.shape[1]
    half, core = block_ref.shape[0], 1 - info_ref[CORE]
    total = total_ref[...] + left_side(core, w_ref, block_ref, lhs)
    users = pl.ds(pl.multiple_of(core * half, half), half)
    weights = w_ref[...].astype(F32)
    count = jnp.sum(jnp.sum(weights, axis=0, keepdims=True), axis=1, keepdims=True)
    inverse = 1.0 / count
    pcol = jnp.sum(total, axis=1, keepdims=True) * inverse
    prow = jnp.broadcast_to(pcol, (P_SIZE, LANES)).T[0:1, :]
    hi, mid, lo = split3(prow)
    chi, cmid, clo = split3(jnp.broadcast_to(count, (1, LANES)))
    rows = [v[:, h : h + LANES] for v in (hi, mid, lo) for h in (0, LANES)]
    lane1 = lax.broadcasted_iota(jnp.int32, (1, LANES), 1)
    last = jnp.where(lane1 < 32, chi, jnp.where(lane1 < 64, cmid, clo))
    fixed = jnp.concatenate(rows + [last, last], axis=0)
    lane = lax.broadcasted_iota(jnp.int32, (1, tile), 1) % LANES
    lane8 = lax.broadcasted_iota(jnp.int32, (EXTRA, LANES), 1)
    row8 = lax.broadcasted_iota(jnp.int32, (EXTRA, LANES), 0)
    per = LANES // BLK
    pieces = tile // BLK

    def whole(t):
        cut = slice(t * tile, (t + 1) * tile)
        return acc_ref[:, cut] + jnp.dot(
            lhs[...], x_ref[users, cut], preferred_element_type=F32
        )

    later = whole(0)
    for t in range(items // tile):
        acc = later
        if t + 1 < items // tile:
            later = whole(t + 1)
        colsum = acc[P_SIZE : P_SIZE + 1, :]
        mrow = colsum * inverse
        moment = acc[0:P_SIZE, :] - pcol * colsum
        top = jnp.max(jnp.max(jnp.abs(moment), axis=0, keepdims=True), axis=1, keepdims=True)
        scale = (8192.0 / jnp.maximum(top, 1e-30)).astype(BF16).astype(F32)
        v = moment * scale
        v3 = v * v * v
        coded = (v3 * v3 * v3).astype(BF16).T.reshape(pieces, BLK, P_SIZE)
        for k in range(pieces):
            place = slot(t * pieces + k)
            out_ref[place, 0:BLK, :] = coded[k, :, 0:LANES]
            out_ref[place, BLK : 2 * BLK, :] = coded[k, :, LANES:]
        hi, mid, lo = split3(mrow)
        base = jnp.where((row8 == 7) & (lane8 >= 96), scale, fixed)
        for q in range(per):
            mix = jnp.where(
                lane < 32,
                pltpu.roll(hi, (tile - 32 * q) % tile, 1),
                jnp.where(
                    lane < 64,
                    pltpu.roll(mid, (tile + 32 - 32 * q) % tile, 1),
                    pltpu.roll(lo, (tile + 64 - 32 * q) % tile, 1),
                ),
            )
            for g in range(tile // LANES):
                row = jnp.broadcast_to(mix[:, g * LANES : (g + 1) * LANES], (EXTRA, LANES))
                stats = jnp.where(row8 == 6, row, base).astype(BF16)
                out_ref[slot(t * pieces + g * per + q), 2 * BLK :, :] = stats


def moments(info, x, mine, other, weights, pieces):
    acc, total = own_half(info, x, mine, weights)
    users, items = x.shape
    tile = 512
    return pl.pallas_call(
        functools.partial(moment_kernel, tile),
        in_specs=[pl.BlockSpec(memory_space=pltpu.SMEM)]
        + [pl.BlockSpec(memory_space=pltpu.VMEM)] * 5,
        out_specs=pl.BlockSpec(memory_space=pltpu.VMEM),
        out_shape=jax.ShapeDtypeStruct((pieces, 2 * BLK + EXTRA, LANES), BF16),
        scratch_shapes=[pltpu.VMEM((P_SIZE + 16, users // CORES), BF16)],
        compiler_params=pltpu.CompilerParams(vmem_limit_bytes=16 * 2**20),
        cost_estimate=pl.CostEstimate(
            flops=users * items * P_SIZE, bytes_accessed=4 * 2**20, transcendentals=0
        ),
    )(info, weights.reshape(-1, LANES), other, x, acc, total)


def merge_kernel(groups, cycles, in_ref, cov_ref, mean_ref):
    stats0 = in_ref[0, :, 2 * BLK :, :].astype(F32)
    part = lambda row: jnp.concatenate([stats0[:, row, :], stats0[:, row + 1, :]], axis=1)
    panel = part(0) + part(2) + part(4)
    last = stats0[:, 7, :]
    count = last[:, 0:1] + last[:, 32:33] + last[:, 64:65]
    everyone = jnp.sum(count, axis=0, keepdims=True)
    share = count / everyone
    panel_dev = panel - jnp.sum(share * panel, axis=0, keepdims=True)
    for i in range(cycles):
        at = i % CORES * (cycles // CORES) + i // CORES
        stats = in_ref[at, :, 2 * BLK :, :].astype(F32)
        row = stats[:, 6, :]
        mean = row[:, 0:32] + row[:, 32:64] + row[:, 64:96]
        mean_all = jnp.sum(share * mean, axis=0, keepdims=True)
        mean_ref[i : i + 1, :] = mean_all
        left = jnp.broadcast_to(share, (groups, 32)) * (mean - mean_all)
        between = lax.dot_general(
            left,
            panel_dev,
            (((0,), (0,)), ((), ())),
            precision=lax.Precision.HIGHEST,
            preferred_element_type=F32,
        )
        back = 1.0 / (everyone * stats[:, 7, 96:97])
        within = jnp.zeros((2 * BLK, LANES), F32)
        for u in range(groups):
            y = in_ref[at, u, 0 : 2 * BLK, :].astype(F32)
            shrink = jnp.exp2((-8.0 / 9.0) * jnp.log2(jnp.maximum(jnp.abs(y), 1e-37)))
            within = within + (y * back[u : u + 1, :]) * shrink
        first = within[0:BLK] + between[:, 0:LANES]
        second = within[BLK:] + between[:, LANES:]
        cov_ref[i, :, 0:LANES] = first
        cov_ref[i, :, LANES:] = second


def merge(pieces, groups, cycles):
    return pl.pallas_call(
        functools.partial(merge_kernel, groups, cycles),
        out_shape=[
            jax.ShapeDtypeStruct((cycles, BLK, P_SIZE), F32),
            jax.ShapeDtypeStruct((cycles, BLK), F32),
        ],
        in_specs=[pl.BlockSpec(memory_space=pltpu.VMEM)],
        out_specs=[pl.BlockSpec(memory_space=pltpu.VMEM)] * 2,
        compiler_params=pltpu.CompilerParams(vmem_limit_bytes=24 * 2**20),
        cost_estimate=pl.CostEstimate(
            flops=20 * 2**20, bytes_accessed=3 * 2**20, transcendentals=2 * 2**20
        ),
    )(pieces.reshape(cycles, groups, *pieces.shape[1:]))


def spread_panel(x, info, core, same, start):
    ring = lax.axis_size(ITEMS)
    chips = ring // CORES
    half = x.shape[0] // CORES
    across = [(i, i ^ 1) for i in range(ring)]

    def step(block, distance):
        pairs = [
            (y * CORES + c, (y + distance) % chips * CORES + c)
            for y in range(chips)
            for c in range(CORES)
        ]
        return lax.ppermute(block, ITEMS, pairs)

    own = lax.dynamic_slice(x, (core * half, start), (half, P_SIZE))
    other = lax.dynamic_slice(x, ((1 - core) * half, start), (half, P_SIZE))
    own, other = lax.optimization_barrier((own, other))
    mine = jnp.where(same, own, lax.ppermute(other, ITEMS, across))
    right, left = step(mine, 1), step(mine, -1)
    first, second = turn(right, left, touch(x, mine, info))
    far_a, far_b = step(first, 1), step(second, -1)
    mine = join(info, mine, right, left, far_a, far_b)
    return mine, lax.ppermute(mine, ITEMS, across)


def per_device(interactions, user_weights, panel_index):
    groups, ring = lax.axis_size(USERS), lax.axis_size(ITEMS)
    me, chips = lax.axis_index(ITEMS), ring // CORES
    per_shard = interactions.shape[1] // P_SIZE
    owner, place = panel_index[0] // per_shard, panel_index[0] % per_shard
    core = me % CORES
    away = (me // CORES - owner // CORES) % chips
    same = core == owner % CORES
    info = jnp.stack([core, away]).astype(jnp.int32)
    mine, other = spread_panel(interactions, info, core, same, place * P_SIZE)
    pieces = moments(info, interactions, mine, other, user_weights, groups * ring)
    moved = lax.all_to_all(pieces, ORDER, 0, 0, tiled=True)
    return tuple(merge(moved, groups, ring))


def solution(mesh):
    split = Mesh(mesh.devices.reshape(4, 4, 4, CORES), USERS + ITEMS)
    return jax.shard_map(
        per_device,
        mesh=split,
        in_specs=(P(USERS, ITEMS), P(USERS), P()),
        out_specs=(P(None, USERS + ITEMS, None), P(None, USERS + ITEMS)),
        check_vma=False,
    )
```

```python
import functools

import jax
import jax.numpy as jnp
from jax import lax
from jax.experimental import pallas as pl
from jax.experimental.pallas import tpu as pltpu
from jax.sharding import Mesh
from jax.sharding import PartitionSpec as P

P_SIZE = 256
BLK = 32
LANES = 128
CORES = 2
USERS, ITEMS = ("z", "x"), ("y", "c")
ORDER = ("c", "y", "x", "z")
CORE, AWAY = range(2)
EXTRA = 8
F32 = jnp.float32
BF16 = jnp.bfloat16


def slot(owner):
    place = dict(zip(USERS + ITEMS, (owner // 32, owner // 8 % 4, owner // 2 % 4, owner % 2)))
    index = 0
    for axis in ORDER:
        index = index * (CORES if axis == "c" else 4) + place[axis]
    return index


def split3(value):
    parts = []
    for _ in range(3):
        part = value.astype(BF16).astype(F32)
        parts.append(part)
        value = value - part
    return parts


def touch_kernel(x_ref, after_ref, info_ref, out_ref):
    out_ref[...] = jnp.zeros_like(out_ref)


def touch(x, *after):
    return pl.pallas_call(
        touch_kernel,
        in_specs=[pl.BlockSpec(memory_space=pltpu.VMEM)] + [pl.BlockSpec(memory_space=pl.ANY)] * 2,
        out_specs=pl.BlockSpec(memory_space=pltpu.VMEM),
        out_shape=jax.ShapeDtypeStruct((8, LANES), F32),
        compiler_params=pltpu.CompilerParams(vmem_limit_bytes=2 * 2**20),
        cost_estimate=pl.CostEstimate(
            flops=0, bytes_accessed=x.size * x.dtype.itemsize, transcendentals=0
        ),
    )(x, *after)


def turn_kernel(right_ref, left_ref, after_ref, first_ref, second_ref):
    part = first_ref.shape[0]
    first_ref[...] = right_ref[0:part, :]
    second_ref[...] = left_ref[part:, :]


def turn(right, left, after):
    rows, columns = right.shape
    shape = jax.ShapeDtypeStruct((rows // 2, columns), right.dtype)
    return pl.pallas_call(
        turn_kernel,
        in_specs=[pl.BlockSpec(memory_space=pltpu.VMEM)] * 2 + [pl.BlockSpec(memory_space=pl.ANY)],
        out_specs=[pl.BlockSpec(memory_space=pltpu.VMEM)] * 2,
        out_shape=[shape, shape],
        compiler_params=pltpu.CompilerParams(vmem_limit_bytes=4 * 2**20),
        cost_estimate=pl.CostEstimate(flops=0, bytes_accessed=2**20, transcendentals=0),
    )(right, left, after)


def join_kernel(info_ref, mine_ref, right_ref, left_ref, far_a_ref, far_b_ref, out_ref):
    part = far_a_ref.shape[0]
    for k, ref in ((0, mine_ref), (1, right_ref), (3, left_ref)):

        @pl.when(info_ref[AWAY] == k)
        def _():
            out_ref[...] = ref[...]

    @pl.when(info_ref[AWAY] == 2)
    def _():
        out_ref[0:part, :] = far_a_ref[...]
        out_ref[part:, :] = far_b_ref[...]


def join(info, *blocks):
    return pl.pallas_call(
        join_kernel,
        in_specs=[pl.BlockSpec(memory_space=pltpu.SMEM)]
        + [pl.BlockSpec(memory_space=pltpu.VMEM)] * len(blocks),
        out_specs=pl.BlockSpec(memory_space=pltpu.VMEM),
        out_shape=jax.ShapeDtypeStruct(blocks[0].shape, blocks[0].dtype),
        compiler_params=pltpu.CompilerParams(vmem_limit_bytes=2 * 2**20),
        cost_estimate=pl.CostEstimate(flops=0, bytes_accessed=2**20, transcendentals=0),
    )(info, *blocks)


def left_side(core, w_ref, block_ref, lhs):
    half = block_ref.shape[0]
    lanes16 = w_ref[...].astype(F32)
    per = half // LANES
    rows = jnp.where(core == 0, lanes16[0:per], lanes16[per:])
    wrow = jnp.concatenate([rows[k : k + 1, :] for k in range(per)], axis=1)
    product = block_ref[...].T.astype(F32) * wrow
    lhs[0:P_SIZE, :] = product.astype(BF16)
    lhs[P_SIZE:, :] = jnp.broadcast_to(wrow, (16, half)).astype(BF16)
    total = product[:, 0:LANES]
    for g in range(LANES, half, LANES):
        total += product[:, g : g + LANES]
    return total


def own_kernel(tile, info_ref, w_ref, block_ref, x_ref, acc_ref, total_ref, lhs):
    half, core = block_ref.shape[0], info_ref[CORE]
    total_ref[...] = left_side(core, w_ref, block_ref, lhs)
    users = pl.ds(pl.multiple_of(core * half, half), half)
    for t in range(x_ref.shape[1] // tile):
        cut = slice(t * tile, (t + 1) * tile)
        acc_ref[:, cut] = jnp.dot(lhs[...], x_ref[users, cut], preferred_element_type=F32)


def own_half(info, x, block, weights):
    users, items = x.shape
    return pl.pallas_call(
        functools.partial(own_kernel, 512),
        in_specs=[pl.BlockSpec(memory_space=pltpu.SMEM)]
        + [pl.BlockSpec(memory_space=pltpu.VMEM)] * 3,
        out_specs=[pl.BlockSpec(memory_space=pltpu.VMEM)] * 2,
        out_shape=[
            jax.ShapeDtypeStruct((P_SIZE + 16, items), F32),
            jax.ShapeDtypeStruct((P_SIZE, LANES), F32),
        ],
        scratch_shapes=[pltpu.VMEM((P_SIZE + 16, users // CORES), BF16)],
        compiler_params=pltpu.CompilerParams(vmem_limit_bytes=12 * 2**20),
        cost_estimate=pl.CostEstimate(
            flops=users * items * P_SIZE, bytes_accessed=4 * 2**20, transcendentals=0
        ),
    )(info, weights.reshape(-1, LANES), block, x)


def moment_kernel(
    tile, info_ref, w_ref, block_ref, x_ref, acc_ref, total_ref, out_ref, lhs
):
    items = x_ref.shape[1]
    half, core = block_ref.shape[0], 1 - info_ref[CORE]
    total = total_ref[...] + left_side(core, w_ref, block_ref, lhs)
    users = pl.ds(pl.multiple_of(core * half, half), half)
    weights = w_ref[...].astype(F32)
    count = jnp.sum(jnp.sum(weights, axis=0, keepdims=True), axis=1, keepdims=True)
    inverse = 1.0 / count
    pcol = jnp.sum(total, axis=1, keepdims=True) * inverse
    prow = jnp.broadcast_to(pcol, (P_SIZE, LANES)).T[0:1, :]
    hi, mid, lo = split3(prow)
    chi, cmid, clo = split3(jnp.broadcast_to(count, (1, LANES)))
    rows = [v[:, h : h + LANES] for v in (hi, mid, lo) for h in (0, LANES)]
    lane1 = lax.broadcasted_iota(jnp.int32, (1, LANES), 1)
    last = jnp.where(lane1 < 32, chi, jnp.where(lane1 < 64, cmid, clo))
    fixed = jnp.concatenate(rows + [last, last], axis=0)
    lane = lax.broadcasted_iota(jnp.int32, (1, tile), 1) % LANES
    lane8 = lax.broadcasted_iota(jnp.int32, (EXTRA, LANES), 1)
    row8 = lax.broadcasted_iota(jnp.int32, (EXTRA, LANES), 0)
    per = LANES // BLK
    pieces = tile // BLK

    def whole(t):
        cut = slice(t * tile, (t + 1) * tile)
        return acc_ref[:, cut] + jnp.dot(
            lhs[...], x_ref[users, cut], preferred_element_type=F32
        )

    later = whole(0)
    for t in range(items // tile):
        acc = later
        if t + 1 < items // tile:
            later = whole(t + 1)
        mrow = acc[P_SIZE : P_SIZE + 1, :] * inverse
        moment = acc[0:P_SIZE, :] * inverse - pcol * mrow
        top = jnp.max(jnp.max(jnp.abs(moment), axis=0, keepdims=True), axis=1, keepdims=True)
        scale = (32768.0 / jnp.maximum(top, 1e-30)).astype(BF16).astype(F32)
        v = moment * scale
        v2 = v * v
        coded = (v * jnp.abs(v) * v2 * (v2 * v2)).astype(BF16).T.reshape(pieces, BLK, P_SIZE)
        for k in range(pieces):
            place = slot(t * pieces + k)
            out_ref[place, 0:BLK, :] = coded[k, :, 0:LANES]
            out_ref[place, BLK : 2 * BLK, :] = coded[k, :, LANES:]
        hi, mid, lo = split3(mrow)
        base = jnp.where((row8 == 7) & (lane8 >= 96), scale, fixed)
        for q in range(per):
            mix = jnp.where(
                lane < 32,
                pltpu.roll(hi, (tile - 32 * q) % tile, 1),
                jnp.where(
                    lane < 64,
                    pltpu.roll(mid, (tile + 32 - 32 * q) % tile, 1),
                    pltpu.roll(lo, (tile + 64 - 32 * q) % tile, 1),
                ),
            )
            for g in range(tile // LANES):
                row = jnp.broadcast_to(mix[:, g * LANES : (g + 1) * LANES], (EXTRA, LANES))
                stats = jnp.where(row8 == 6, row, base).astype(BF16)
                out_ref[slot(t * pieces + g * per + q), 2 * BLK :, :] = stats


def moments(info, x, mine, other, weights, pieces):
    acc, total = own_half(info, x, mine, weights)
    users, items = x.shape
    tile = 512
    return pl.pallas_call(
        functools.partial(moment_kernel, tile),
        in_specs=[pl.BlockSpec(memory_space=pltpu.SMEM)]
        + [pl.BlockSpec(memory_space=pltpu.VMEM)] * 5,
        out_specs=pl.BlockSpec(memory_space=pltpu.VMEM),
        out_shape=jax.ShapeDtypeStruct((pieces, 2 * BLK + EXTRA, LANES), BF16),
        scratch_shapes=[pltpu.VMEM((P_SIZE + 16, users // CORES), BF16)],
        compiler_params=pltpu.CompilerParams(vmem_limit_bytes=16 * 2**20),
        cost_estimate=pl.CostEstimate(
            flops=users * items * P_SIZE, bytes_accessed=4 * 2**20, transcendentals=0
        ),
    )(info, weights.reshape(-1, LANES), other, x, acc, total)


def merge_kernel(groups, cycles, in_ref, cov_ref, mean_ref):
    stats0 = in_ref[0, :, 2 * BLK :, :].astype(F32)
    part = lambda row: jnp.concatenate([stats0[:, row, :], stats0[:, row + 1, :]], axis=1)
    panel = part(0) + part(2) + part(4)
    last = stats0[:, 7, :]
    count = last[:, 0:1] + last[:, 32:33] + last[:, 64:65]
    share = count / jnp.sum(count, axis=0, keepdims=True)
    panel_dev = panel - jnp.sum(share * panel, axis=0, keepdims=True)
    for i in range(cycles):
        at = i % CORES * (cycles // CORES) + i // CORES
        stats = in_ref[at, :, 2 * BLK :, :].astype(F32)
        row = stats[:, 6, :]
        mean = row[:, 0:32] + row[:, 32:64] + row[:, 64:96]
        mean_all = jnp.sum(share * mean, axis=0, keepdims=True)
        mean_ref[i : i + 1, :] = mean_all
        left = jnp.broadcast_to(share, (groups, 32)) * (mean - mean_all)
        between = lax.dot_general(
            left,
            panel_dev,
            (((0,), (0,)), ((), ())),
            precision=lax.Precision.HIGHEST,
            preferred_element_type=F32,
        )
        back = share / stats[:, 7, 96:97]
        within = jnp.zeros((2 * BLK, LANES), F32)
        for u in range(groups):
            y = in_ref[at, u, 0 : 2 * BLK, :].astype(F32)
            shrink = jnp.exp2(-0.875 * jnp.log2(jnp.maximum(jnp.abs(y), 1e-37)))
            within = within + (y * back[u : u + 1, :]) * shrink
        first = within[0:BLK] + between[:, 0:LANES]
        second = within[BLK:] + between[:, LANES:]
        cov_ref[i, :, 0:LANES] = first
        cov_ref[i, :, LANES:] = second


def merge(pieces, groups, cycles):
    return pl.pallas_call(
        functools.partial(merge_kernel, groups, cycles),
        out_shape=[
            jax.ShapeDtypeStruct((cycles, BLK, P_SIZE), F32),
            jax.ShapeDtypeStruct((cycles, BLK), F32),
        ],
        in_specs=[pl.BlockSpec(memory_space=pltpu.VMEM)],
        out_specs=[pl.BlockSpec(memory_space=pltpu.VMEM)] * 2,
        compiler_params=pltpu.CompilerParams(vmem_limit_bytes=24 * 2**20),
        cost_estimate=pl.CostEstimate(
            flops=20 * 2**20, bytes_accessed=3 * 2**20, transcendentals=2 * 2**20
        ),
    )(pieces.reshape(cycles, groups, *pieces.shape[1:]))


def spread_panel(x, info, core, same, start):
    ring = lax.axis_size(ITEMS)
    chips = ring // CORES
    half = x.shape[0] // CORES
    across = [(i, i ^ 1) for i in range(ring)]

    def step(block, distance):
        pairs = [
            (y * CORES + c, (y + distance) % chips * CORES + c)
            for y in range(chips)
            for c in range(CORES)
        ]
        return lax.ppermute(block, ITEMS, pairs)

    own = lax.dynamic_slice(x, (core * half, start), (half, P_SIZE))
    other = lax.dynamic_slice(x, ((1 - core) * half, start), (half, P_SIZE))
    own = lax.optimization_barrier(own)
    mine = jnp.where(same, own, lax.ppermute(other, ITEMS, across))
    right, left = step(mine, 1), step(mine, -1)
    first, second = turn(right, left, touch(x, mine, info))
    far_a, far_b = step(first, 1), step(second, -1)
    mine = join(info, mine, right, left, far_a, far_b)
    return mine, lax.ppermute(mine, ITEMS, across)


def per_device(interactions, user_weights, panel_index):
    groups, ring = lax.axis_size(USERS), lax.axis_size(ITEMS)
    me, chips = lax.axis_index(ITEMS), ring // CORES
    per_shard = interactions.shape[1] // P_SIZE
    owner, place = panel_index[0] // per_shard, panel_index[0] % per_shard
    core = me % CORES
    away = (me // CORES - owner // CORES) % chips
    same = core == owner % CORES
    info = jnp.stack([core, away]).astype(jnp.int32)
    mine, other = spread_panel(interactions, info, core, same, place * P_SIZE)
    pieces = moments(info, interactions, mine, other, user_weights, groups * ring)
    moved = lax.all_to_all(pieces, ORDER, 0, 0, tiled=True)
    return tuple(merge(moved, groups, ring))


def solution(mesh):
    split = Mesh(mesh.devices.reshape(4, 4, 4, CORES), USERS + ITEMS)
    return jax.shard_map(
        per_device,
        mesh=split,
        in_specs=(P(USERS, ITEMS), P(USERS), P()),
        out_specs=(P(None, USERS + ITEMS, None), P(None, USERS + ITEMS)),
        check_vma=False,
    )
```
